32 devices in a mesh: expert: 8 (over z, y), half: 4 (over x, core).
Axes of the slice: x: 2, y: 2, z: 4, core: 2. Of those that a mesh axis runs over, the one named last changes fastest.
Arguments:
- tokens: bfloat16 [1568, 1024], P('expert', 'half'), may hold values from -128 to 128
- slot_params: bfloat16 [1024, 16], P('half'), may hold values from -0.5 to 0.5
- w_up: bfloat16 [8, 1024, 4096], P('expert', None, 'half'), may hold values from -0.1875 to 0.1875
- w_down: bfloat16 [8, 4096, 1024], P('expert', 'half'), may hold values from -0.09375 to 0.09375
- cotangent: bfloat16 [1568, 1024], P('expert', 'half'), may hold values from -6 to 6
Outputs:
- mixed: bfloat16 [1568, 1024], P('expert', 'half')
- grad_tokens: bfloat16 [1568, 1024], P('expert', 'half')
- grad_params: float32 [1024, 16], P('half')
The draws below stay inside these ranges and needn't reach their ends.
All inputs are finite; a program needn't handle non-finite values.
Results may differ from the reference program's by a relative error of at most 0.017.
Values may be sent and summed in bfloat16 or wider, within the bound.
No kernel may reach another device: no remote copies, remote signals or barrier semaphores. Data moves between devices by JAX's collectives and lax.ppermute only.
A program may use at most 64 MiB of HBM per device.

```python
import math
import jax
import jax.numpy as jnp
from jax import lax

D = 1024
MLP_DIM = 4096
SEQ = 196
SLOTS = 2
EXPERTS = 8
COLUMNS = 16
IMAGES = 8
TOKENS = 1568
N_HALF = 4


def shared_draw(key):
    subkeys = [jax.random.fold_in(key, 101 + offset) for offset in range(9)]
    normals = jnp.clip(jax.random.normal(subkeys[0], (D, COLUMNS), jnp.float32), -4.0, 4.0)
    column_scale = jnp.exp(jax.random.uniform(subkeys[1], (1, COLUMNS), jnp.float32, math.log(0.5), math.log(4.0)))
    slot_matrix = (normals * column_scale / math.sqrt(D)).astype(jnp.bfloat16).astype(jnp.float32)
    gaussian = jnp.clip(jax.random.normal(subkeys[2], (IMAGES, SEQ, D), jnp.float32), -5.0, 5.0)
    row_scale = jnp.exp(jax.random.uniform(subkeys[3], (IMAGES, SEQ, 1), jnp.float32, math.log(0.5), math.log(4.0)))
    image_tokens = row_scale * gaussian
    return (slot_matrix, image_tokens.reshape(TOKENS, D))


def draw_tokens(key, part):
    return shared_draw(key)[1].astype(jnp.bfloat16)


def draw_slot_params(key, part):
    return shared_draw(key)[0].astype(jnp.bfloat16)


def block_scale(rng, shape, pieces, smallest, largest):
    level, own = 1.0, jax.random.fold_in(rng, 6)
    for position, blocks in pieces:
        draws = jnp.exp(jax.random.uniform(jax.random.fold_in(own, position), (blocks,), jnp.float32, smallest / len(pieces), largest / len(pieces)))
        level = level * jnp.repeat(draws, shape[position] // blocks).reshape([-1 if axis == position else 1 for axis in range(len(shape))])
    return level


def scatter_about(key, shape, width, most, pieces=(), kind=jnp.bfloat16):
    entries = width * jax.random.normal(key, shape, jnp.float32)
    if pieces:
        entries = entries * block_scale(key, shape, pieces, -0.22, 0.18)
    return jnp.clip(entries, -most, most).astype(kind)


def setup_inputs(seed: int = 0) -> dict:
    seeds = jax.random.split(jax.random.key(seed), 6)
    return {
        "tokens": draw_tokens(jax.random.fold_in(seeds[5], 71), 0),
        "slot_params": draw_slot_params(jax.random.fold_in(seeds[5], 71), 0),
        "w_up": scatter_about(seeds[2], (EXPERTS, D, MLP_DIM), D ** -0.5, 0.1875, ((0, 8), (2, 4))),
        "w_down": scatter_about(seeds[3], (EXPERTS, MLP_DIM, D), MLP_DIM ** -0.5, 0.09375, ((0, 8), (1, 4))),
        "cotangent": scatter_about(seeds[4], (TOKENS, D), 1.0, 6.0, ((0, 8), (1, 4))),
    }


def gelu_grad(preact, upstream):
    pullback = jax.vjp(jax.nn.gelu, preact)[1]
    return pullback(upstream)[0]

def softmax_back(probabilities, upstream, over_axis):
    inner = lax.optimization_barrier(jnp.sum(probabilities * upstream, axis=over_axis, keepdims=True))
    return probabilities * (upstream - inner)

def rounded_sum(partials):
    rounded = lax.optimization_barrier(partials.astype(jnp.bfloat16))
    return lax.optimization_barrier(jnp.sum(rounded.astype(jnp.float32), axis=0)).astype(jnp.bfloat16)

def expert_rows(operands):
    slot_rows, grad_rows, up_matrix, down_matrix = operands
    block_width = MLP_DIM // N_HALF
    row_count = slot_rows.shape[0]
    up_wide = up_matrix.astype(jnp.float32)
    down_wide = down_matrix.astype(jnp.float32)
    preact = jnp.dot(slot_rows.astype(jnp.float32), up_wide)
    hidden = jax.nn.gelu(preact).astype(jnp.bfloat16)
    partial_out = jnp.einsum('rhk,hkd->hrd', hidden.astype(jnp.float32).reshape(row_count, N_HALF, block_width), down_wide.reshape(N_HALF, block_width, D))
    slot_out = rounded_sum(partial_out)
    grad_hidden = jnp.dot(grad_rows.astype(jnp.float32), down_wide.T)
    grad_preact = gelu_grad(preact, grad_hidden).astype(jnp.bfloat16)
    partial_in = jnp.einsum('rhk,dhk->hrd', grad_preact.astype(jnp.float32).reshape(row_count, N_HALF, block_width), up_wide.reshape(D, N_HALF, block_width))
    grad_slot_in = rounded_sum(partial_in)
    return (slot_out, grad_slot_in)

def to_experts(per_image):
    grouped = per_image.reshape(IMAGES, EXPERTS, SLOTS, D)
    return jnp.transpose(grouped, (1, 0, 2, 3)).reshape(EXPERTS, IMAGES * SLOTS, D)

def from_experts(per_expert):
    grouped = per_expert.reshape(EXPERTS, IMAGES, SLOTS, D)
    return jnp.transpose(grouped, (1, 0, 2, 3)).reshape(IMAGES, COLUMNS, D)

def reference(tokens, slot_params, w_up, w_down, cotangent):
    inputs = tokens.reshape(IMAGES, SEQ, D).astype(jnp.float32)
    upstream = cotangent.reshape(IMAGES, SEQ, D).astype(jnp.float32)
    params_wide = slot_params.astype(jnp.float32)
    logits = jnp.einsum('imd,dc->imc', inputs, params_wide)
    dispatch = jax.nn.softmax(logits, axis=1)
    combine = jax.nn.softmax(logits, axis=2)
    dispatch_bf = dispatch.astype(jnp.bfloat16)
    combine_bf = combine.astype(jnp.bfloat16)
    slot_in = jnp.einsum('imc,imd->icd', dispatch_bf.astype(jnp.float32), inputs).astype(jnp.bfloat16)
    grad_slot_out = jnp.einsum('imc,imd->icd', combine_bf.astype(jnp.float32), upstream).astype(jnp.bfloat16)
    expert_out, expert_grad = lax.map(expert_rows, (to_experts(slot_in), to_experts(grad_slot_out), w_up, w_down))
    slot_out = from_experts(expert_out).astype(jnp.float32)
    grad_slot_in = from_experts(expert_grad).astype(jnp.float32)
    mixed = jnp.einsum('imc,icd->imd', combine_bf.astype(jnp.float32), slot_out).astype(jnp.bfloat16)
    grad_combine = jnp.einsum('imd,icd->imc', upstream, slot_out)
    grad_dispatch = jnp.einsum('imd,icd->imc', inputs, grad_slot_in)
    grad_logits = softmax_back(combine, grad_combine, 2) + softmax_back(dispatch, grad_dispatch, 1)
    grad_logit_bf = grad_logits.astype(jnp.bfloat16).astype(jnp.float32)
    grad_tokens = jnp.einsum('imc,icd->imd', dispatch_bf.astype(jnp.float32), grad_slot_in) + jnp.einsum('imc,dc->imd', grad_logit_bf, params_wide)
    grad_params = jnp.einsum('imd,imc->dc', inputs, grad_logit_bf)
    return (mixed.reshape(TOKENS, D), grad_tokens.astype(jnp.bfloat16).reshape(TOKENS, D), grad_params)
```

```python
import jax
import jax.numpy as jnp
from jax import lax
from jax.sharding import Mesh, PartitionSpec as P

F32 = jnp.float32
BF16 = jnp.bfloat16


def swap(array, axis):
    return lax.ppermute(array, axis, [(0, 1), (1, 0)])


def dot(left, right, over):
    return lax.dot_general(left, right, ((over[:1], over[1:]), ((), ())), preferred_element_type=F32)


def softmax(logits, axis):
    shifted = jnp.exp(logits - jnp.max(logits, axis=axis, keepdims=True))
    return shifted / jnp.sum(shifted, axis=axis, keepdims=True)


def softmax_back(probabilities, upstream, axis):
    inner = jnp.sum(probabilities * upstream, axis=axis, keepdims=True)
    return probabilities * (upstream - inner)


def gelu_grad(preact, upstream):
    pullback = jax.vjp(jax.nn.gelu, preact)[1]
    return pullback(upstream)[0]


def local(experts, halves, tokens, slot_params, w_up, w_down, cotangent):
    seq, quarter = tokens.shape
    columns = slot_params.shape[1]
    slots = columns // experts
    x_size = halves // 2
    half = lax.axis_index("x") * 2 + lax.axis_index("core")
    up_matrix, down_matrix = w_up[0], w_down[0]

    logits = dot(slot_params, tokens, (0, 1))
    logits = logits + swap(logits, "core")
    logits = logits + swap(logits, "x")
    both = jnp.stack([tokens, cotangent])
    across = swap(both, "x")
    beside = swap(jnp.stack([both, across]), "core")
    dispatch = softmax(logits, 1)
    combine = softmax(logits, 0)
    dispatch_bf = dispatch.astype(BF16)
    combine_bf = combine.astype(BF16)
    slot_in = dot(dispatch_bf, tokens, (1, 0)).astype(BF16).reshape(experts, 1, slots, quarter)
    grad_out = dot(combine_bf, cotangent, (1, 0)).astype(BF16).reshape(experts, 1, slots, quarter)
    rows = jnp.concatenate([slot_in, grad_out], axis=1).reshape(1, experts, 2 * slots, quarter)
    rows = jnp.broadcast_to(rows, (halves, experts, 2 * slots, quarter)).reshape(halves * experts, 2 * slots, quarter)

    got = lax.all_to_all(rows, ("x", "core", "expert"), 0, 0, tiled=True)
    got = got.reshape(halves, experts, 2, slots, quarter)
    forward = got[:, :, 0].reshape(halves, experts * slots, quarter)
    backward = got[:, :, 1].reshape(halves, experts * slots, quarter)
    forward = jnp.transpose(forward, (1, 0, 2)).reshape(experts * slots, halves * quarter)
    backward = jnp.transpose(backward, (1, 0, 2)).reshape(experts * slots, halves * quarter)
    preact = dot(forward, up_matrix, (1, 0))
    hidden = jax.nn.gelu(preact).astype(BF16)
    out_part = dot(hidden, down_matrix, (1, 0)).astype(BF16)
    grad_hidden = dot(backward, down_matrix, (1, 1))
    grad_preact = gelu_grad(preact, grad_hidden).astype(BF16)
    in_part = dot(grad_preact, up_matrix, (1, 1)).astype(BF16)
    part = jnp.stack([out_part.reshape(experts, slots, -1), in_part.reshape(experts, slots, -1)], axis=1)
    part = part.reshape(experts, 2 * slots, halves * quarter)

    pair = (part.astype(F32) + swap(part, "core").astype(F32)).astype(BF16)
    pair = jnp.broadcast_to(pair[None], (x_size,) + pair.shape).reshape(x_size * experts, 2 * slots, halves * quarter)
    back = lax.all_to_all(pair, ("x", "expert"), 0, 0, tiled=True)
    back = back.reshape(x_size, experts, 2, slots, halves, quarter).astype(F32).sum(0).astype(BF16)
    slot_out = back[:, 0].reshape(columns, halves, quarter)
    grad_in = back[:, 1].reshape(columns, halves, quarter)

    grad_combine = grad_dispatch = 0.0
    parts = (both, beside[0], across, beside[1])
    for offset, (token_part, cotangent_part) in enumerate(parts):
        which = jnp.bitwise_xor(half, offset)
        grad_combine += dot(lax.dynamic_index_in_dim(slot_out, which, 1, False), cotangent_part, (1, 1))
        grad_dispatch += dot(lax.dynamic_index_in_dim(grad_in, which, 1, False), token_part, (1, 1))
    grad_logits = softmax_back(combine, grad_combine, 0) + softmax_back(dispatch, grad_dispatch, 1)
    grad_logit_bf = grad_logits.astype(BF16)

    params_part = dot(grad_logit_bf, tokens, (1, 0)).astype(BF16)
    params_part = jnp.broadcast_to(params_part[None], (experts,) + params_part.shape)
    params_parts = lax.all_to_all(params_part, "expert", 0, 0, tiled=True)
    grad_params = params_parts.astype(F32).sum(0).T

    own_out = lax.dynamic_index_in_dim(slot_out, half, 1, False)
    own_in = lax.dynamic_index_in_dim(grad_in, half, 1, False)
    mixed = dot(combine_bf, own_out, (0, 0)).astype(BF16)
    grad_tokens = (dot(dispatch_bf, own_in, (0, 0)) + dot(grad_logit_bf, slot_params, (0, 1))).astype(BF16)
    return mixed, grad_tokens, grad_params


def solution(mesh):
    experts, halves = mesh.shape["expert"], mesh.shape["half"]
    split = Mesh(mesh.devices.reshape(experts, halves // 2, 2), ("expert", "x", "core"))
    half = ("x", "core")
    in_specs = (
        P("expert", half),
        P(half, None),
        P("expert", None, half),
        P("expert", half, None),
        P("expert", half),
    )
    out_specs = (P("expert", half), P("expert", half), P(half, None))

    def program(*args):
        return jax.shard_map(
            lambda *blocks: local(experts, halves, *blocks),
            mesh=split,
            in_specs=in_specs,
            out_specs=out_specs,
            check_vma=False,
        )(*args)

    return program
```

```python
import functools

import jax
import jax.numpy as jnp
from jax import lax
from jax.experimental import pallas as pl
from jax.experimental.pallas import tpu as pltpu
from jax.sharding import Mesh, PartitionSpec as P

F32 = jnp.float32
BF16 = jnp.bfloat16
MIB = 2**20


def swap(array, axis):
    return lax.ppermute(array, axis, [(0, 1), (1, 0)])


def dot(left, right, over):
    return lax.dot_general(left, right, ((over[:1], over[1:]), ((), ())), preferred_element_type=F32)


def softmax(logits, axis):
    shifted = jnp.exp(logits - jnp.max(logits, axis=axis, keepdims=True))
    return shifted / jnp.sum(shifted, axis=axis, keepdims=True)


def softmax_back(probabilities, upstream, axis):
    inner = jnp.sum(probabilities * upstream, axis=axis, keepdims=True)
    return probabilities * (upstream - inner)


def gelu_parts(value):
    scale, cubic = 0.7978845608028654, 0.044715
    square = value * value
    curve = jnp.tanh(scale * (value + cubic * value * square))
    slope = 0.5 * (1.0 + curve) + 0.5 * value * (1.0 - curve * curve) * scale * (1.0 + 3.0 * cubic * square)
    return 0.5 * value * (1.0 + curve), slope


def inward(table, slots, lead):
    table = table.reshape(-1, slots, table.shape[1]).swapaxes(0, 1)
    table = jnp.concatenate([table[:, lead:], table[:, :lead]], axis=1)
    return table.reshape(-1, table.shape[2])


def outward(table, slots, lead):
    table = table.reshape(slots, -1, table.shape[1])
    lead = table.shape[1] - lead
    table = jnp.concatenate([table[:, lead:], table[:, :lead]], axis=1)
    return table.swapaxes(0, 1).reshape(-1, table.shape[2])


def to_blocks(forward, backward, slots, copies):
    rows = [part for table in (forward, backward) for part in jnp.split(table.astype(F32), slots)]
    blocks = jnp.stack(rows, axis=1).astype(BF16)
    return jnp.concatenate([blocks] * copies, axis=0)


def from_blocks(blocks, slots):
    rows = [blocks[:, i] for i in range(2 * slots)]
    return jnp.concatenate(rows[:slots], axis=0), jnp.concatenate(rows[slots:], axis=0)


def start_kernel(slots, lead, tokens, cotangent, params, own, params_in, logits, params_here, sems):
    copies = [
        pltpu.make_async_copy(source, target, sems.at[i])
        for i, (source, target) in enumerate(((params, params_here), (tokens, own.at[0]), (cotangent, own.at[1])))
    ]
    for copy in copies:
        copy.start()
    copies[0].wait()
    params_in[...] = inward(params_here[...].astype(F32), slots, lead).astype(BF16)
    copies[1].wait()
    logits[...] = dot(params_in[...], own[0], (1, 1))
    copies[2].wait()


def weight_kernel(after, up_matrix, down_matrix, up_here, down_here, sems):
    copies = [
        pltpu.make_async_copy(source, target, sems.at[i])
        for i, (source, target) in enumerate(((up_matrix, up_here), (down_matrix, down_here)))
    ]
    for copy in copies:
        copy.start()
    for copy in copies:
        copy.wait()


def slot_kernel(slots, x_size, first, second, own, beside, blocks, dispatch, combine):
    logits = first[...] + second[...]
    over_tokens, over_columns = softmax(logits, 1), softmax(logits, 0)
    dispatch[...] = over_tokens
    combine[...] = over_columns
    quarter = own.shape[2]
    for part, core in ((own, lax.axis_index("core")), (beside, 1 - lax.axis_index("core"))):
        here = pl.ds(pl.multiple_of(core * quarter, quarter), quarter)
        slot_in = dot(over_tokens.astype(BF16), part[0], (1, 0))
        grad_out = dot(over_columns.astype(BF16), part[1], (1, 0))
        blocks[:, :, here] = to_blocks(slot_in, grad_out, slots, x_size)


def expert_kernel(slots, x_size, blocks, up_matrix, down_matrix, sums):
    got = blocks[...].astype(F32)
    sides = [from_blocks(part, slots) for part in jnp.split(got, x_size)]
    forward, backward = (jnp.concatenate(side, axis=1).astype(BF16) for side in zip(*sides))
    preact = dot(forward, up_matrix[0], (1, 0))
    grad_hidden = dot(backward, down_matrix[0], (1, 1))
    hidden, slope = gelu_parts(preact)
    sums[0] = dot(hidden.astype(BF16), down_matrix[0], (1, 0)).astype(BF16)
    sums[1] = dot((grad_hidden * slope).astype(BF16), up_matrix[0], (1, 1)).astype(BF16)


def pair_kernel(slots, x_size, first, second, blocks):
    total = first[...].astype(F32) + second[...].astype(F32)
    blocks[...] = to_blocks(total[0], total[1], slots, x_size)


def image_kernel(
    slots, x_size, lead, blocks, own, beside, across, corner, dispatch, combine, params, params_part, mixed, grad_tokens, rows
):
    half = lax.axis_index("x") * 2 + lax.axis_index("core")
    quarter = own.shape[2]
    slot_out, grad_in = from_blocks(sum(jnp.split(blocks[...].astype(F32), x_size)), slots)
    rows[0] = slot_out.astype(BF16)
    rows[1] = grad_in.astype(BF16)
    grad_combine = grad_dispatch = 0.0
    for offset, part in enumerate((own, beside, across, corner)):
        start = pl.multiple_of(jnp.bitwise_xor(half, offset) * quarter, quarter)
        grad_combine += dot(rows[0, :, pl.ds(start, quarter)], part[1], (1, 1))
        grad_dispatch += dot(rows[1, :, pl.ds(start, quarter)], part[0], (1, 1))
    grad_logits = softmax_back(combine[...], grad_combine, 0) + softmax_back(dispatch[...], grad_dispatch, 1)
    partial = dot(grad_logits.astype(BF16), own[0], (1, 0))
    partial = outward(partial, slots, lead).astype(BF16)
    params_part[...] = jnp.broadcast_to(partial[None], params_part.shape)
    here = pl.ds(pl.multiple_of(half * quarter, quarter), quarter)
    mixed[...] = dot(combine[...].astype(BF16), rows[0, :, here], (0, 0)).astype(BF16)
    token_term = dot(dispatch[...].astype(BF16), rows[1, :, here], (0, 0))
    grad_tokens[...] = (token_term + dot(grad_logits.astype(BF16), params[...], (0, 0))).astype(BF16)


def end_kernel(parts, mixed_here, grad_tokens_here, mixed, grad_tokens, grad_params):
    mixed[...] = mixed_here[...]
    grad_tokens[...] = grad_tokens_here[...]
    grad_params[...] = jnp.sum(parts[...].astype(F32), axis=0)


def call(kernel, outs, *args, scratch=(), in_hbm=(), limit=16):
    whole = pl.BlockSpec(memory_space=pltpu.VMEM)
    elsewhere = pl.BlockSpec(memory_space=pltpu.HBM)
    run = pl.pallas_call(
        kernel,
        out_shape=[jax.ShapeDtypeStruct(*out) if isinstance(out, tuple) else out for out in outs],
        in_specs=[elsewhere if i in in_hbm else whole for i in range(len(args))],
        out_specs=[whole] * len(outs),
        scratch_shapes=list(scratch),
        compiler_params=pltpu.CompilerParams(vmem_limit_bytes=limit * MIB),
    )
    return run(*(pltpu.with_memory_space_constraint(arg, pltpu.HBM) if i in in_hbm else arg for i, arg in enumerate(args)))


def local(experts, halves, tokens, slot_params, w_up, w_down, cotangent):
    seq, quarter = tokens.shape
    columns = slot_params.shape[1]
    slots = columns // experts
    x_size = halves // 2
    width = halves * quarter
    table = (columns, seq)
    lead = experts * 5 // 8
    order = [(lead + i) % experts for i in range(experts)]
    wide_order = [expert * x_size + x for x in range(x_size) for expert in order]

    own, params, logits = call(
        functools.partial(start_kernel, slots, lead),
        [((2, seq, quarter), BF16), ((columns, quarter), BF16), (table, F32)],
        tokens,
        cotangent,
        slot_params.T,
        scratch=[pltpu.VMEM((columns, quarter), BF16), pltpu.SemaphoreType.DMA((3,))],
        in_hbm=(0, 1, 2),
    )
    logits = logits + swap(logits, "core")
    other = swap(logits, "x")
    across = swap(own, "x")
    beside = swap(own, "core")
    up_here, down_here = call(
        weight_kernel,
        [pltpu.VMEM(w_up.shape, BF16), pltpu.VMEM(w_down.shape, BF16)],
        logits,
        w_up,
        w_down,
        scratch=[pltpu.SemaphoreType.DMA((2,))],
        in_hbm=(1, 2),
    )
    logits, up_here, down_here = lax.optimization_barrier((logits, up_here, down_here))
    blocks, dispatch, combine = call(
        functools.partial(slot_kernel, slots, x_size),
        [((x_size * experts, 2 * slots, 2 * quarter), BF16), (table, F32), (table, F32)],
        logits,
        other,
        own,
        beside,
    )

    blocks = lax.all_to_all(blocks, ("expert", "x"), 0, 0, tiled=True, axis_index_groups=[wide_order])
    (sums,) = call(
        functools.partial(expert_kernel, slots, x_size), [((2, columns, width), BF16)], blocks, up_here, down_here
    )

    sums, across = lax.optimization_barrier((sums, across))
    other_sums = swap(sums, "core")
    corner = swap(across, "core")
    (blocks,) = call(
        functools.partial(pair_kernel, slots, x_size),
        [((x_size * experts, 2 * slots, width), BF16)],
        sums,
        other_sums,
    )
    blocks, corner = lax.optimization_barrier((blocks, corner))
    blocks = lax.all_to_all(blocks, ("expert", "x"), 0, 0, tiled=True, axis_index_groups=[wide_order])
    params_part, mixed, grad_tokens = call(
        functools.partial(image_kernel, slots, x_size, lead),
        [((experts, columns, quarter), BF16), pltpu.VMEM((seq, quarter), BF16), pltpu.VMEM((seq, quarter), BF16)],
        blocks,
        own,
        beside,
        across,
        corner,
        dispatch,
        combine,
        params,
        scratch=[pltpu.VMEM((2, columns, width), BF16)],
        limit=16 if experts * columns <= 1024 else 48,
    )

    params_parts = lax.all_to_all(params_part, "expert", 0, 0, tiled=True, axis_index_groups=[order])
    mixed, grad_tokens, grad_params = call(
        end_kernel,
        [((seq, quarter), BF16), ((seq, quarter), BF16), ((columns, quarter), F32)],
        params_parts,
        mixed,
        grad_tokens,
        limit=16 if experts * columns <= 1024 else 48,
    )
    return mixed, grad_tokens, grad_params.T


def solution(mesh):
    experts, halves = mesh.shape["expert"], mesh.shape["half"]
    split = Mesh(mesh.devices.reshape(experts, halves // 2, 2), ("expert", "x", "core"))
    half = ("x", "core")
    in_specs = (
        P("expert", half),
        P(half, None),
        P("expert", None, half),
        P("expert", half, None),
        P("expert", half),
    )
    out_specs = (P("expert", half), P("expert", half), P(half, None))

    def program(*args):
        return jax.shard_map(
            lambda *blocks: local(experts, halves, *blocks),
            mesh=split,
            in_specs=in_specs,
            out_specs=out_specs,
            check_vma=False,
        )(*args)

    return program
```

```python
import functools

import jax
import jax.numpy as jnp
from jax import lax
from jax.experimental import pallas as pl
from jax.experimental.pallas import tpu as pltpu
from jax.sharding import Mesh, PartitionSpec as P

F32 = jnp.float32
BF16 = jnp.bfloat16
MIB = 2**20


def swap(array, axis):
    return lax.ppermute(array, axis, [(0, 1), (1, 0)])


def dot(left, right, over):
    return lax.dot_general(left, right, ((over[:1], over[1:]), ((), ())), preferred_element_type=F32)


def softmax(logits, axis):
    shifted = jnp.exp(logits - jnp.max(logits, axis=axis, keepdims=True))
    return shifted / jnp.sum(shifted, axis=axis, keepdims=True)


def softmax_back(probabilities, upstream, axis):
    inner = jnp.sum(probabilities * upstream, axis=axis, keepdims=True)
    return probabilities * (upstream - inner)


def gelu_parts(value):
    scale, cubic = 0.7978845608028654, 0.044715
    square = value * value
    curve = jnp.tanh(scale * (value + cubic * value * square))
    slope = 0.5 * (1.0 + curve) + 0.5 * value * (1.0 - curve * curve) * scale * (1.0 + 3.0 * cubic * square)
    return 0.5 * value * (1.0 + curve), slope


def inward(table, slots, lead):
    table = table.reshape(-1, slots, table.shape[1]).swapaxes(0, 1)
    table = jnp.concatenate([table[:, lead:], table[:, :lead]], axis=1)
    return table.reshape(-1, table.shape[2])


def outward(table, slots, lead):
    table = table.reshape(slots, -1, table.shape[1])
    lead = table.shape[1] - lead
    table = jnp.concatenate([table[:, lead:], table[:, :lead]], axis=1)
    return table.swapaxes(0, 1).reshape(-1, table.shape[2])


def to_blocks(forward, backward, slots, copies):
    rows = [part for table in (forward, backward) for part in jnp.split(table.astype(F32), slots)]
    blocks = jnp.stack(rows, axis=1).astype(BF16)
    return jnp.concatenate([blocks] * copies, axis=0)


def from_blocks(blocks, slots):
    rows = [blocks[:, i] for i in range(2 * slots)]
    return jnp.concatenate(rows[:slots], axis=0), jnp.concatenate(rows[slots:], axis=0)


def start_kernel(slots, lead, tokens, cotangent, params, own, params_in, logits, params_here, sems):
    copies = [
        pltpu.make_async_copy(source, target, sems.at[i])
        for i, (source, target) in enumerate(((params, params_here), (tokens, own.at[0]), (cotangent, own.at[1])))
    ]
    for copy in copies:
        copy.start()
    copies[0].wait()
    params_in[...] = inward(params_here[...].astype(F32), slots, lead).astype(BF16)
    copies[1].wait()
    logits[...] = dot(params_in[...], own[0], (1, 1))
    copies[2].wait()


def weight_kernel(after, up_matrix, down_matrix, up_here, down_here, sems):
    copies = [
        pltpu.make_async_copy(source, target, sems.at[i])
        for i, (source, target) in enumerate(((up_matrix, up_here), (down_matrix, down_here)))
    ]
    for copy in copies:
        copy.start()
    for copy in copies:
        copy.wait()


def slot_kernel(slots, x_size, first, second, own, beside, blocks, dispatch, combine):
    logits = first[...] + second[...]
    over_tokens, over_columns = softmax(logits, 1), softmax(logits, 0)
    dispatch[...] = over_tokens
    combine[...] = over_columns
    quarter = own.shape[2]
    for part, core in ((own, lax.axis_index("core")), (beside, 1 - lax.axis_index("core"))):
        here = pl.ds(pl.multiple_of(core * quarter, quarter), quarter)
        slot_in = dot(over_tokens.astype(BF16), part[0], (1, 0))
        grad_out = dot(over_columns.astype(BF16), part[1], (1, 0))
        blocks[:, :, here] = to_blocks(slot_in, grad_out, slots, x_size)


def expert_kernel(slots, x_size, blocks, up_matrix, down_matrix, sums):
    got = blocks[...].astype(F32)
    sides = [from_blocks(part, slots) for part in jnp.split(got, x_size)]
    forward, backward = (jnp.concatenate(side, axis=1).astype(BF16) for side in zip(*sides))
    preact = dot(forward, up_matrix[0], (1, 0))
    grad_hidden = dot(backward, down_matrix[0], (1, 1))
    hidden, slope = gelu_parts(preact)
    sums[0] = dot(hidden.astype(BF16), down_matrix[0], (1, 0)).astype(BF16)
    sums[1] = dot((grad_hidden * slope).astype(BF16), up_matrix[0], (1, 1)).astype(BF16)


def pair_kernel(slots, x_size, first, second, blocks):
    total = first[...].astype(F32) + second[...].astype(F32)
    blocks[...] = to_blocks(total[0], total[1], slots, x_size)


def image_kernel(
    slots, x_size, lead, blocks, own, beside, across, corner, dispatch, combine, params, params_part, mixed, grad_tokens, rows
):
    half = lax.axis_index("x") * 2 + lax.axis_index("core")
    quarter = own.shape[2]
    slot_out, grad_in = from_blocks(sum(jnp.split(blocks[...].astype(F32), x_size)), slots)
    rows[0] = slot_out.astype(BF16)
    rows[1] = grad_in.astype(BF16)
    grad_combine = grad_dispatch = 0.0
    for offset, part in enumerate((own, beside, across, corner)):
        start = pl.multiple_of(jnp.bitwise_xor(half, offset) * quarter, quarter)
        grad_combine += dot(rows[0, :, pl.ds(start, quarter)], part[1], (1, 1))
        grad_dispatch += dot(rows[1, :, pl.ds(start, quarter)], part[0], (1, 1))
    grad_logits = softmax_back(combine[...], grad_combine, 0) + softmax_back(dispatch[...], grad_dispatch, 1)
    partial = dot(grad_logits.astype(BF16), own[0], (1, 0))
    partial = outward(partial, slots, lead).astype(BF16)
    params_part[...] = jnp.broadcast_to(partial[None], params_part.shape)
    here = pl.ds(pl.multiple_of(half * quarter, quarter), quarter)
    mixed[...] = dot(combine[...].astype(BF16), rows[0, :, here], (0, 0)).astype(BF16)
    token_term = dot(dispatch[...].astype(BF16), rows[1, :, here], (0, 0))
    grad_tokens[...] = (token_term + dot(grad_logits.astype(BF16), params[...], (0, 0))).astype(BF16)


def end_kernel(parts, mixed_here, grad_tokens_here, mixed, grad_tokens, grad_params):
    mixed[...] = mixed_here[...]
    grad_tokens[...] = grad_tokens_here[...]
    grad_params[...] = jnp.sum(parts[...].astype(F32), axis=0)


def call(kernel, outs, *args, scratch=(), in_hbm=(), limit=16):
    whole = pl.BlockSpec(memory_space=pltpu.VMEM)
    elsewhere = pl.BlockSpec(memory_space=pltpu.HBM)
    run = pl.pallas_call(
        kernel,
        out_shape=[jax.ShapeDtypeStruct(*out) if isinstance(out, tuple) else out for out in outs],
        in_specs=[elsewhere if i in in_hbm else whole for i in range(len(args))],
        out_specs=[whole] * len(outs),
        scratch_shapes=list(scratch),
        compiler_params=pltpu.CompilerParams(vmem_limit_bytes=limit * MIB),
    )
    return run(*(pltpu.with_memory_space_constraint(arg, pltpu.HBM) if i in in_hbm else arg for i, arg in enumerate(args)))


def local(experts, halves, tokens, slot_params, w_up, w_down, cotangent):
    seq, quarter = tokens.shape
    columns = slot_params.shape[1]
    slots = columns // experts
    x_size = halves // 2
    width = halves * quarter
    table = (columns, seq)
    lead = experts * 5 // 8
    order = [(lead + i) % experts for i in range(experts)]
    wide_order = [expert * x_size + x for x in range(x_size) for expert in order]

    own, params, logits = call(
        functools.partial(start_kernel, slots, lead),
        [((2, seq, quarter), BF16), ((columns, quarter), BF16), (table, F32)],
        tokens,
        cotangent,
        slot_params.T,
        scratch=[pltpu.VMEM((columns, quarter), BF16), pltpu.SemaphoreType.DMA((3,))],
        in_hbm=(0, 1, 2),
    )
    other = swap(logits, "x")
    beside = swap(own, "core")
    up_here, down_here = call(
        weight_kernel,
        [pltpu.VMEM(w_up.shape, BF16), pltpu.VMEM(w_down.shape, BF16)],
        logits,
        w_up,
        w_down,
        scratch=[pltpu.SemaphoreType.DMA((2,))],
        in_hbm=(1, 2),
    )
    logits, up_here, down_here = lax.optimization_barrier((logits + other, up_here, down_here))
    logits, own_later = lax.optimization_barrier((logits, own))
    across = swap(own_later, "x")
    other = swap(logits, "core")
    blocks, dispatch, combine = call(
        functools.partial(slot_kernel, slots, x_size),
        [((x_size * experts, 2 * slots, 2 * quarter), BF16), (table, F32), (table, F32)],
        logits,
        other,
        own,
        beside,
    )

    blocks = lax.all_to_all(blocks, ("expert", "x"), 0, 0, tiled=True, axis_index_groups=[wide_order])
    (sums,) = call(
        functools.partial(expert_kernel, slots, x_size), [((2, columns, width), BF16)], blocks, up_here, down_here
    )

    sums, across = lax.optimization_barrier((sums, across))
    other_sums = swap(sums, "core")
    corner = swap(across, "core")
    (blocks,) = call(
        functools.partial(pair_kernel, slots, x_size),
        [((x_size * experts, 2 * slots, width), BF16)],
        sums,
        other_sums,
    )
    blocks, corner = lax.optimization_barrier((blocks, corner))
    blocks = lax.all_to_all(blocks, ("expert", "x"), 0, 0, tiled=True, axis_index_groups=[wide_order])
    params_part, mixed, grad_tokens = call(
        functools.partial(image_kernel, slots, x_size, lead),
        [((experts, columns, quarter), BF16), pltpu.VMEM((seq, quarter), BF16), pltpu.VMEM((seq, quarter), BF16)],
        blocks,
        own,
        beside,
        across,
        corner,
        dispatch,
        combine,
        params,
        scratch=[pltpu.VMEM((2, columns, width), BF16)],
        limit=16 if experts * columns <= 1024 else 48,
    )

    params_parts = lax.all_to_all(params_part, "expert", 0, 0, tiled=True, axis_index_groups=[order])
    mixed, grad_tokens, grad_params = call(
        end_kernel,
        [((seq, quarter), BF16), ((seq, quarter), BF16), ((columns, quarter), F32)],
        params_parts,
        mixed,
        grad_tokens,
        limit=16 if experts * columns <= 1024 else 48,
    )
    return mixed, grad_tokens, grad_params.T


def solution(mesh):
    experts, halves = mesh.shape["expert"], mesh.shape["half"]
    split = Mesh(mesh.devices.reshape(experts, halves // 2, 2), ("expert", "x", "core"))
    half = ("x", "core")
    in_specs = (
        P("expert", half),
        P(half, None),
        P("expert", None, half),
        P("expert", half, None),
        P("expert", half),
    )
    out_specs = (P("expert", half), P("expert", half), P(half, None))

    def program(*args):
        return jax.shard_map(
            lambda *blocks: local(experts, halves, *blocks),
            mesh=split,
            in_specs=in_specs,
            out_specs=out_specs,
            check_vma=False,
        )(*args)

    return program
```

```python
import functools

import jax
import jax.numpy as jnp
from jax import lax
from jax.experimental import pallas as pl
from jax.experimental.pallas import tpu as pltpu
from jax.sharding import Mesh, PartitionSpec as P

F32 = jnp.float32
BF16 = jnp.bfloat16
MIB = 2**20


def swap(array, axis):
    return lax.ppermute(array, axis, [(0, 1), (1, 0)])


def dot(left, right, over):
    return lax.dot_general(left, right, ((over[:1], over[1:]), ((), ())), preferred_element_type=F32)


def softmax(logits, axis):
    shifted = jnp.exp(logits - jnp.max(logits, axis=axis, keepdims=True))
    return shifted / jnp.sum(shifted, axis=axis, keepdims=True)


def softmax_back(probabilities, upstream, axis):
    inner = jnp.sum(probabilities * upstream, axis=axis, keepdims=True)
    return probabilities * (upstream - inner)


def gelu_parts(value):
    scale, cubic = 0.7978845608028654, 0.044715
    square = value * value
    curve = jnp.tanh(scale * (value + cubic * value * square))
    slope = 0.5 * (1.0 + curve) + 0.5 * value * (1.0 - curve * curve) * scale * (1.0 + 3.0 * cubic * square)
    return 0.5 * value * (1.0 + curve), slope


def inward(table, slots, lead):
    table = table.reshape(-1, slots, table.shape[1]).swapaxes(0, 1)
    table = jnp.concatenate([table[:, lead:], table[:, :lead]], axis=1)
    return table.reshape(-1, table.shape[2])


def outward(table, slots, lead):
    table = table.reshape(slots, -1, table.shape[1])
    lead = table.shape[1] - lead
    table = jnp.concatenate([table[:, lead:], table[:, :lead]], axis=1)
    return table.swapaxes(0, 1).reshape(-1, table.shape[2])


def to_blocks(forward, backward, slots, copies):
    rows = [part for table in (forward, backward) for part in jnp.split(table.astype(F32), slots)]
    blocks = jnp.stack(rows, axis=1).astype(BF16)
    return jnp.concatenate([blocks] * copies, axis=0)


def from_blocks(blocks, slots):
    rows = [blocks[:, i] for i in range(2 * slots)]
    return jnp.concatenate(rows[:slots], axis=0), jnp.concatenate(rows[slots:], axis=0)


def start_kernel(slots, lead, tokens, cotangent, params, own, params_in, logits, params_here, sems):
    copies = [
        pltpu.make_async_copy(source, target, sems.at[i])
        for i, (source, target) in enumerate(((params, params_here), (tokens, own.at[0]), (cotangent, own.at[1])))
    ]
    for copy in copies:
        copy.start()
    copies[0].wait()
    params_in[...] = inward(params_here[...].astype(F32), slots, lead).astype(BF16)
    copies[1].wait()
    logits[...] = dot(params_in[...], own[0], (1, 1))
    copies[2].wait()


def weight_kernel(chunks, after, up_matrix, down_matrix, up_here, down_here, up_turned, down_turned, sems):
    sides = ((up_matrix, up_here, up_turned), (down_matrix, down_here, down_turned))
    copies = []
    for i, (source, target, _) in enumerate(sides):
        step = source.shape[1] // chunks
        for j in range(chunks):
            part = pl.ds(j * step, step)
            copies.append(pltpu.make_async_copy(source.at[0, part], target.at[part], sems.at[i * chunks + j]))
            copies[-1].start()
    for i, (_, target, turned) in enumerate(sides):
        step = target.shape[0] // chunks
        for j in range(chunks):
            copies[i * chunks + j].wait()
            turned[:, j * step : (j + 1) * step] = target[j * step : (j + 1) * step].T


def slot_kernel(slots, x_size, first, second, own, beside, blocks, dispatch, combine):
    logits = first[...] + second[...]
    over_tokens, over_columns = softmax(logits, 1), softmax(logits, 0)
    dispatch[...] = over_tokens
    combine[...] = over_columns
    quarter = own.shape[2]
    for part, core in ((own, lax.axis_index("core")), (beside, 1 - lax.axis_index("core"))):
        here = pl.ds(pl.multiple_of(core * quarter, quarter), quarter)
        slot_in = dot(over_tokens.astype(BF16), part[0], (1, 0))
        grad_out = dot(over_columns.astype(BF16), part[1], (1, 0))
        blocks[:, :, here] = to_blocks(slot_in, grad_out, slots, x_size)


def expert_kernel(slots, x_size, blocks, up_matrix, down_matrix, up_turned, down_turned, sums):
    got = blocks[...].astype(F32)
    first, second = jnp.split(got, x_size)
    in_order = lax.axis_index("x") != lax.axis_index("core")
    parts = (jnp.where(in_order, first, second), jnp.where(in_order, second, first))
    sides = [from_blocks(part, slots) for part in parts]
    forward, backward = (jnp.concatenate(side, axis=1).astype(BF16) for side in zip(*sides))
    preact = dot(forward, up_matrix[...], (1, 0))
    grad_hidden = dot(backward, down_turned[...], (1, 0))
    hidden, slope = gelu_parts(preact)
    sums[0] = dot(hidden.astype(BF16), down_matrix[...], (1, 0)).astype(BF16)
    sums[1] = dot((grad_hidden * slope).astype(BF16), up_turned[...], (1, 0)).astype(BF16)


def pair_kernel(slots, x_size, first, second, blocks):
    total = first[...].astype(F32) + second[...].astype(F32)
    blocks[...] = to_blocks(total[0], total[1], slots, x_size)


def image_kernel(
    slots, x_size, lead, blocks, own, beside, across, corner, dispatch, combine, params, params_part, mixed, grad_tokens, rows
):
    half = lax.axis_index("x") * 2 + lax.axis_index("core")
    quarter = own.shape[2]
    slot_out, grad_in = from_blocks(sum(jnp.split(blocks[...].astype(F32), x_size)), slots)
    rows[0] = slot_out.astype(BF16)
    rows[1] = grad_in.astype(BF16)
    grad_combine = grad_dispatch = 0.0
    for offset, part in enumerate((own, beside, across, corner)):
        start = pl.multiple_of(jnp.bitwise_xor(half, offset) * quarter, quarter)
        grad_combine += dot(rows[0, :, pl.ds(start, quarter)], part[1], (1, 1))
        grad_dispatch += dot(rows[1, :, pl.ds(start, quarter)], part[0], (1, 1))
    grad_logits = softmax_back(combine[...], grad_combine, 0) + softmax_back(dispatch[...], grad_dispatch, 1)
    partial = [dot(grad_logits.astype(BF16), part[0], (1, 0)) for part in (own, beside)]
    upper = lax.axis_index("core") == 1
    for i, part in enumerate((jnp.where(upper, *partial), jnp.where(upper, *partial[::-1]))):
        count = params_part.shape[0] // 2
        part = outward(part, slots, lead).astype(BF16)
        params_part[i * count : (i + 1) * count] = jnp.broadcast_to(part[None], (count, *part.shape))
    here = pl.ds(pl.multiple_of(half * quarter, quarter), quarter)
    mixed[...] = dot(combine[...].astype(BF16), rows[0, :, here], (0, 0)).astype(BF16)
    token_term = dot(dispatch[...].astype(BF16), rows[1, :, here], (0, 0))
    grad_tokens[...] = (token_term + dot(grad_logits.astype(BF16), params[...], (0, 0))).astype(BF16)


def end_kernel(parts, mixed_here, grad_tokens_here, mixed, grad_tokens, grad_params):
    mixed[...] = mixed_here[...]
    grad_tokens[...] = grad_tokens_here[...]
    grad_params[...] = jnp.sum(parts[...].astype(F32), axis=0)


def call(kernel, outs, *args, scratch=(), in_hbm=(), limit=16):
    whole = pl.BlockSpec(memory_space=pltpu.VMEM)
    elsewhere = pl.BlockSpec(memory_space=pltpu.HBM)
    run = pl.pallas_call(
        kernel,
        out_shape=[jax.ShapeDtypeStruct(*out) if isinstance(out, tuple) else out for out in outs],
        in_specs=[elsewhere if i in in_hbm else whole for i in range(len(args))],
        out_specs=[whole] * len(outs),
        scratch_shapes=list(scratch),
        compiler_params=pltpu.CompilerParams(vmem_limit_bytes=limit * MIB),
    )
    return run(*(pltpu.with_memory_space_constraint(arg, pltpu.HBM) if i in in_hbm else arg for i, arg in enumerate(args)))


def local(experts, halves, tokens, slot_params, w_up, w_down, cotangent):
    seq, quarter = tokens.shape
    columns = slot_params.shape[1]
    slots = columns // experts
    x_size = halves // 2
    width = halves * quarter
    table = (columns, seq)
    lead, middle = experts * 5 // 8, experts // 2
    order = [(lead + i) % experts for i in range(experts)]
    near = [list(range(middle))[::-1], list(range(middle, experts))]
    wide = [
        [(expert * x_size + (x if core else 1 - x)) * 2 + core for core in (1, 0) for expert in order]
        for x in range(x_size)
    ]
    narrow = [
        [(image * x_size + x) * 2 + core for core in (1, 0) for image in near[side if core else 1 - side]]
        for x in range(x_size)
        for side in (0, 1)
    ]
    axes = ("expert", "x", "core")

    own, params, logits = call(
        functools.partial(start_kernel, slots, lead),
        [((2, seq, quarter), BF16), ((columns, quarter), BF16), (table, F32)],
        tokens,
        cotangent,
        slot_params.T,
        scratch=[pltpu.VMEM((columns, quarter), BF16), pltpu.SemaphoreType.DMA((3,))],
        in_hbm=(0, 1, 2),
    )
    other = swap(logits, "x")
    beside = swap(own, "core")
    chunks = 2
    shapes = [w_up.shape[1:], w_down.shape[1:], w_up.shape[:0:-1], w_down.shape[:0:-1]]
    weights = call(
        functools.partial(weight_kernel, chunks),
        [pltpu.VMEM(shape, BF16) for shape in shapes],
        logits,
        w_up,
        w_down,
        scratch=[pltpu.SemaphoreType.DMA((2 * chunks,))],
        in_hbm=(1, 2),
    )
    logits, *weights = lax.optimization_barrier((logits + other, *weights))
    logits, own_later = lax.optimization_barrier((logits, own))
    across = swap(own_later, "x")
    other = swap(logits, "core")
    blocks, dispatch, combine = call(
        functools.partial(slot_kernel, slots, x_size),
        [((x_size * experts, 2 * slots, 2 * quarter), BF16), (table, F32), (table, F32)],
        logits,
        other,
        own,
        beside,
    )

    blocks = lax.all_to_all(blocks, axes, 0, 0, tiled=True, axis_index_groups=wide)
    (sums,) = call(
        functools.partial(expert_kernel, slots, x_size), [((2, columns, width), BF16)], blocks, *weights
    )

    sums, across = lax.optimization_barrier((sums, across))
    other_sums = swap(sums, "core")
    corner = swap(across, "core")
    (blocks,) = call(
        functools.partial(pair_kernel, slots, x_size),
        [((x_size * experts, 2 * slots, width), BF16)],
        sums,
        other_sums,
    )
    blocks, corner = lax.optimization_barrier((blocks, corner))
    blocks = lax.all_to_all(blocks, axes, 0, 0, tiled=True, axis_index_groups=wide)
    params_part, mixed, grad_tokens = call(
        functools.partial(image_kernel, slots, x_size, lead),
        [((experts, columns, quarter), BF16), pltpu.VMEM((seq, quarter), BF16), pltpu.VMEM((seq, quarter), BF16)],
        blocks,
        own,
        beside,
        across,
        corner,
        dispatch,
        combine,
        params,
        scratch=[pltpu.VMEM((2, columns, width), BF16)],
        limit=16 if experts * columns <= 1024 else 48,
    )

    params_parts = lax.all_to_all(params_part, axes, 0, 0, tiled=True, axis_index_groups=narrow)
    mixed, grad_tokens, grad_params = call(
        end_kernel,
        [((seq, quarter), BF16), ((seq, quarter), BF16), ((columns, quarter), F32)],
        params_parts,
        mixed,
        grad_tokens,
        limit=16 if experts * columns <= 1024 else 48,
    )
    return mixed, grad_tokens, grad_params.T


def solution(mesh):
    experts, halves = mesh.shape["expert"], mesh.shape["half"]
    split = Mesh(mesh.devices.reshape(experts, halves // 2, 2), ("expert", "x", "core"))
    half = ("x", "core")
    in_specs = (
        P("expert", half),
        P(half, None),
        P("expert", None, half),
        P("expert", half, None),
        P("expert", half),
    )
    out_specs = (P("expert", half), P("expert", half), P(half, None))

    def program(*args):
        return jax.shard_map(
            lambda *blocks: local(experts, halves, *blocks),
            mesh=split,
            in_specs=in_specs,
            out_specs=out_specs,
            check_vma=False,
        )(*args)

    return program
```

```python
import functools

import jax
import jax.numpy as jnp
from jax import lax
from jax.experimental import pallas as pl
from jax.experimental.pallas import tpu as pltpu
from jax.sharding import Mesh, PartitionSpec as P

F32 = jnp.float32
BF16 = jnp.bfloat16
MIB = 2**20


def swap(array, axis):
    return lax.ppermute(array, axis, [(0, 1), (1, 0)])


def dot(left, right, over):
    return lax.dot_general(left, right, ((over[:1], over[1:]), ((), ())), preferred_element_type=F32)


def softmax(logits, axis):
    shifted = jnp.exp(logits - jnp.max(logits, axis=axis, keepdims=True))
    return shifted / jnp.sum(shifted, axis=axis, keepdims=True)


def softmax_back(probabilities, upstream, axis):
    inner = jnp.sum(probabilities * upstream, axis=axis, keepdims=True)
    return probabilities * (upstream - inner)


def gelu_parts(value):
    scale, cubic = 0.7978845608028654, 0.044715
    square = value * value
    curve = jnp.tanh(scale * (value + cubic * value * square))
    slope = 0.5 * (1.0 + curve) + 0.5 * value * (1.0 - curve * curve) * scale * (1.0 + 3.0 * cubic * square)
    return 0.5 * value * (1.0 + curve), slope


def inward(table, slots, lead):
    table = table.reshape(-1, slots, table.shape[1]).swapaxes(0, 1)
    table = jnp.concatenate([table[:, lead:], table[:, :lead]], axis=1)
    return table.reshape(-1, table.shape[2])


def outward(table, slots, lead):
    table = table.reshape(slots, -1, table.shape[1])
    lead = table.shape[1] - lead
    table = jnp.concatenate([table[:, lead:], table[:, :lead]], axis=1)
    return table.swapaxes(0, 1).reshape(-1, table.shape[2])


def to_blocks(forward, backward, slots, copies):
    rows = [part for table in (forward, backward) for part in jnp.split(table.astype(F32), slots)]
    blocks = jnp.stack(rows, axis=1).astype(BF16)
    return jnp.concatenate([blocks] * copies, axis=0)


def from_blocks(blocks, slots):
    rows = [blocks[:, i] for i in range(2 * slots)]
    return jnp.concatenate(rows[:slots], axis=0), jnp.concatenate(rows[slots:], axis=0)


def start_kernel(slots, lead, tokens, cotangent, params, own, params_in, logits, params_here, sems):
    copies = [
        pltpu.make_async_copy(source, target, sems.at[i])
        for i, (source, target) in enumerate(((params, params_here), (tokens, own.at[0]), (cotangent, own.at[1])))
    ]
    for copy in copies:
        copy.start()
    copies[0].wait()
    params_in[...] = inward(params_here[...].astype(F32), slots, lead).astype(BF16)
    copies[1].wait()
    logits[...] = dot(params_in[...], own[0], (1, 1))
    copies[2].wait()


def add_kernel(slots, lead, logits, tokens, params, total):
    params_in = inward(params[...].astype(F32), slots, lead).astype(BF16)
    total[...] = logits[...] + dot(params_in, tokens[...], (1, 1))


def weight_kernel(chunks, after, up_matrix, down_matrix, up_here, down_here, up_turned, down_turned, sems):
    sides = ((up_matrix, up_here, up_turned), (down_matrix, down_here, down_turned))
    copies = []
    for i, (source, target, _) in enumerate(sides):
        step = source.shape[1] // chunks
        for j in range(chunks):
            part = pl.ds(j * step, step)
            copies.append(pltpu.make_async_copy(source.at[0, part], target.at[part], sems.at[i * chunks + j]))
            copies[-1].start()
    for i, (_, target, turned) in enumerate(sides):
        step = target.shape[0] // chunks
        for j in range(chunks):
            copies[i * chunks + j].wait()
            turned[:, j * step : (j + 1) * step] = target[j * step : (j + 1) * step].T


def slot_kernel(slots, x_size, first, second, own, tokens, cotangent, blocks, dispatch, combine):
    logits = first[...] + second[...]
    over_tokens, over_columns = softmax(logits, 1), softmax(logits, 0)
    dispatch[...] = over_tokens
    combine[...] = over_columns
    quarter = own.shape[2]
    core = lax.axis_index("core")
    for part, core in (((own[0], own[1]), core), ((tokens[...], cotangent[...]), 1 - core)):
        here = pl.ds(pl.multiple_of(core * quarter, quarter), quarter)
        slot_in = dot(over_tokens.astype(BF16), part[0], (1, 0))
        grad_out = dot(over_columns.astype(BF16), part[1], (1, 0))
        blocks[:, :, here] = to_blocks(slot_in, grad_out, slots, x_size)


def expert_kernel(slots, x_size, blocks, up_matrix, down_matrix, up_turned, down_turned, sums):
    got = blocks[...].astype(F32)
    first, second = jnp.split(got, x_size)
    in_order = lax.axis_index("x") != lax.axis_index("core")
    parts = (jnp.where(in_order, first, second), jnp.where(in_order, second, first))
    sides = [from_blocks(part, slots) for part in parts]
    forward, backward = (jnp.concatenate(side, axis=1).astype(BF16) for side in zip(*sides))
    preact = dot(forward, up_matrix[...], (1, 0))
    grad_hidden = dot(backward, down_turned[...], (1, 0))
    hidden, slope = gelu_parts(preact)
    sums[0] = dot(hidden.astype(BF16), down_matrix[...], (1, 0)).astype(BF16)
    sums[1] = dot((grad_hidden * slope).astype(BF16), up_turned[...], (1, 0)).astype(BF16)


def pair_kernel(slots, x_size, first, second, blocks):
    total = first[...].astype(F32) + second[...].astype(F32)
    blocks[...] = to_blocks(total[0], total[1], slots, x_size)


def image_kernel(
    slots, x_size, lead, blocks, own, tokens, cotangent, across, corner, dispatch, combine, params, params_part, mixed, grad_tokens, rows
):
    half = lax.axis_index("x") * 2 + lax.axis_index("core")
    quarter = own.shape[2]
    slot_out, grad_in = from_blocks(sum(jnp.split(blocks[...].astype(F32), x_size)), slots)
    rows[0] = slot_out.astype(BF16)
    rows[1] = grad_in.astype(BF16)
    grad_combine = grad_dispatch = 0.0
    for offset, part in enumerate((own, (tokens, cotangent), across, corner)):
        start = pl.multiple_of(jnp.bitwise_xor(half, offset) * quarter, quarter)
        grad_combine += dot(rows[0, :, pl.ds(start, quarter)], part[1][...], (1, 1))
        grad_dispatch += dot(rows[1, :, pl.ds(start, quarter)], part[0][...], (1, 1))
    grad_logits = softmax_back(combine[...], grad_combine, 0) + softmax_back(dispatch[...], grad_dispatch, 1)
    partial = [dot(grad_logits.astype(BF16), part[0], (1, 0)) for part in (own, (tokens[...],))]
    upper = lax.axis_index("core") == 1
    for i, part in enumerate((jnp.where(upper, *partial), jnp.where(upper, *partial[::-1]))):
        count = params_part.shape[0] // 2
        part = outward(part, slots, lead).astype(BF16)
        params_part[i * count : (i + 1) * count] = jnp.broadcast_to(part[None], (count, *part.shape))
    here = pl.ds(pl.multiple_of(half * quarter, quarter), quarter)
    mixed[...] = dot(combine[...].astype(BF16), rows[0, :, here], (0, 0)).astype(BF16)
    token_term = dot(dispatch[...].astype(BF16), rows[1, :, here], (0, 0))
    grad_tokens[...] = (token_term + dot(grad_logits.astype(BF16), params[...], (0, 0))).astype(BF16)


def end_kernel(parts, mixed_here, grad_tokens_here, mixed, grad_tokens, grad_params):
    mixed[...] = mixed_here[...]
    grad_tokens[...] = grad_tokens_here[...]
    grad_params[...] = jnp.sum(parts[...].astype(F32), axis=0)


def call(kernel, outs, *args, scratch=(), in_hbm=(), limit=16):
    whole = pl.BlockSpec(memory_space=pltpu.VMEM)
    elsewhere = pl.BlockSpec(memory_space=pltpu.HBM)
    run = pl.pallas_call(
        kernel,
        out_shape=[jax.ShapeDtypeStruct(*out) if isinstance(out, tuple) else out for out in outs],
        in_specs=[elsewhere if i in in_hbm else whole for i in range(len(args))],
        out_specs=[whole] * len(outs),
        scratch_shapes=list(scratch),
        compiler_params=pltpu.CompilerParams(vmem_limit_bytes=limit * MIB),
    )
    return run(*(pltpu.with_memory_space_constraint(arg, pltpu.HBM) if i in in_hbm else arg for i, arg in enumerate(args)))


def local(experts, halves, tokens, slot_params, w_up, w_down, cotangent):
    seq, quarter = tokens.shape
    columns = slot_params.shape[1]
    slots = columns // experts
    x_size = halves // 2
    width = halves * quarter
    table = (columns, seq)
    lead, middle = experts * 5 // 8, experts // 2
    order = [(lead + i) % experts for i in range(experts)]
    near = [list(range(middle))[::-1], list(range(middle, experts))]
    wide = [
        [(expert * x_size + (x if core else 1 - x)) * 2 + core for core in (1, 0) for expert in order]
        for x in range(x_size)
    ]
    narrow = [
        [(image * x_size + x) * 2 + core for core in (1, 0) for image in near[side if core else 1 - side]]
        for x in range(x_size)
        for side in (0, 1)
    ]
    axes = ("expert", "x", "core")

    beside = [swap(tokens, "core"), swap(cotangent, "core")]
    own, params, logits = call(
        functools.partial(start_kernel, slots, lead),
        [((2, seq, quarter), BF16), ((columns, quarter), BF16), (table, F32)],
        tokens,
        cotangent,
        slot_params.T,
        scratch=[pltpu.VMEM((columns, quarter), BF16), pltpu.SemaphoreType.DMA((3,))],
        in_hbm=(0, 1, 2),
    )
    (logits,) = call(
        functools.partial(add_kernel, slots, lead), [(table, F32)], logits, beside[0], swap(slot_params.T, "core")
    )
    other = swap(logits, "x")
    chunks = 2
    shapes = [w_up.shape[1:], w_down.shape[1:], w_up.shape[:0:-1], w_down.shape[:0:-1]]
    weights = call(
        functools.partial(weight_kernel, chunks),
        [pltpu.VMEM(shape, BF16) for shape in shapes],
        logits,
        w_up,
        w_down,
        scratch=[pltpu.SemaphoreType.DMA((2 * chunks,))],
        in_hbm=(1, 2),
    )
    other, own_later, *weights = lax.optimization_barrier((other, own, *weights))
    across = swap(own_later, "x")
    blocks, dispatch, combine = call(
        functools.partial(slot_kernel, slots, x_size),
        [((x_size * experts, 2 * slots, 2 * quarter), BF16), (table, F32), (table, F32)],
        logits,
        other,
        own,
        *beside,
    )

    blocks = lax.all_to_all(blocks, axes, 0, 0, tiled=True, axis_index_groups=wide)
    (sums,) = call(
        functools.partial(expert_kernel, slots, x_size), [((2, columns, width), BF16)], blocks, *weights
    )

    sums, across = lax.optimization_barrier((sums, across))
    other_sums = swap(sums, "core")
    corner = swap(across, "core")
    (blocks,) = call(
        functools.partial(pair_kernel, slots, x_size),
        [((x_size * experts, 2 * slots, width), BF16)],
        sums,
        other_sums,
    )
    blocks, corner = lax.optimization_barrier((blocks, corner))
    blocks = lax.all_to_all(blocks, axes, 0, 0, tiled=True, axis_index_groups=wide)
    params_part, mixed, grad_tokens = call(
        functools.partial(image_kernel, slots, x_size, lead),
        [((experts, columns, quarter), BF16), pltpu.VMEM((seq, quarter), BF16), pltpu.VMEM((seq, quarter), BF16)],
        blocks,
        own,
        *beside,
        across,
        corner,
        dispatch,
        combine,
        params,
        scratch=[pltpu.VMEM((2, columns, width), BF16)],
        limit=16 if experts * columns <= 1024 else 48,
    )

    params_parts = lax.all_to_all(params_part, axes, 0, 0, tiled=True, axis_index_groups=narrow)
    mixed, grad_tokens, grad_params = call(
        end_kernel,
        [((seq, quarter), BF16), ((seq, quarter), BF16), ((columns, quarter), F32)],
        params_parts,
        mixed,
        grad_tokens,
        limit=16 if experts * columns <= 1024 else 48,
    )
    return mixed, grad_tokens, grad_params.T


def solution(mesh):
    experts, halves = mesh.shape["expert"], mesh.shape["half"]
    split = Mesh(mesh.devices.reshape(experts, halves // 2, 2), ("expert", "x", "core"))
    half = ("x", "core")
    in_specs = (
        P("expert", half),
        P(half, None),
        P("expert", None, half),
        P("expert", half, None),
        P("expert", half),
    )
    out_specs = (P("expert", half), P("expert", half), P(half, None))

    def program(*args):
        return jax.shard_map(
            lambda *blocks: local(experts, halves, *blocks),
            mesh=split,
            in_specs=in_specs,
            out_specs=out_specs,
            check_vma=False,
        )(*args)

    return program
```

```python
import functools

import jax
import jax.numpy as jnp
from jax import lax
from jax.experimental import pallas as pl
from jax.experimental.pallas import tpu as pltpu
from jax.sharding import Mesh, PartitionSpec as P

F32 = jnp.float32
BF16 = jnp.bfloat16
MIB = 2**20


def swap(array, axis):
    return lax.ppermute(array, axis, [(0, 1), (1, 0)])


def dot(left, right, over):
    return lax.dot_general(left, right, ((over[:1], over[1:]), ((), ())), preferred_element_type=F32)


def softmax(logits, axis):
    shifted = jnp.exp(logits - jnp.max(logits, axis=axis, keepdims=True))
    return shifted / jnp.sum(shifted, axis=axis, keepdims=True)


def softmax_back(probabilities, upstream, axis):
    inner = jnp.sum(probabilities * upstream, axis=axis, keepdims=True)
    return probabilities * (upstream - inner)


def gelu_parts(value):
    scale, cubic = 0.7978845608028654, 0.044715
    square = value * value
    curve = jnp.tanh(scale * (value + cubic * value * square))
    slope = 0.5 * (1.0 + curve) + 0.5 * value * (1.0 - curve * curve) * scale * (1.0 + 3.0 * cubic * square)
    return 0.5 * value * (1.0 + curve), slope


def inward(table, slots, lead):
    table = table.reshape(-1, slots, table.shape[1]).swapaxes(0, 1)
    table = jnp.concatenate([table[:, lead:], table[:, :lead]], axis=1)
    return table.reshape(-1, table.shape[2])


def outward(table, slots, lead):
    table = table.reshape(slots, -1, table.shape[1])
    lead = table.shape[1] - lead
    table = jnp.concatenate([table[:, lead:], table[:, :lead]], axis=1)
    return table.swapaxes(0, 1).reshape(-1, table.shape[2])


def to_blocks(forward, backward, slots, copies):
    rows = [part for table in (forward, backward) for part in jnp.split(table.astype(F32), slots)]
    blocks = jnp.stack(rows, axis=1).astype(BF16)
    return jnp.concatenate([blocks] * copies, axis=0)


def from_blocks(blocks, slots):
    rows = [blocks[:, i] for i in range(2 * slots)]
    return jnp.concatenate(rows[:slots], axis=0), jnp.concatenate(rows[slots:], axis=0)


def start_kernel(slots, lead, tokens, cotangent, params, own, params_in, logits, params_here, sems):
    copies = [
        pltpu.make_async_copy(source, target, sems.at[i])
        for i, (source, target) in enumerate(((params, params_here), (tokens, own.at[0]), (cotangent, own.at[1])))
    ]
    for copy in copies:
        copy.start()
    copies[0].wait()
    params_in[...] = inward(params_here[...].astype(F32), slots, lead).astype(BF16)
    copies[1].wait()
    logits[...] = dot(params_in[...], own[0], (1, 1))
    copies[2].wait()


def add_kernel(slots, lead, logits, tokens, params, total):
    params_in = inward(params[...].astype(F32), slots, lead).astype(BF16)
    total[...] = logits[...] + dot(params_in, tokens[...], (1, 1))


def weight_kernel(chunks, after, up_matrix, down_matrix, up_here, down_here, up_turned, down_turned, sems):
    sides = ((up_matrix, up_here, up_turned), (down_matrix, down_here, down_turned))
    copies = []
    for i, (source, target, _) in enumerate(sides):
        step = source.shape[1] // chunks
        for j in range(chunks):
            part = pl.ds(j * step, step)
            copies.append(pltpu.make_async_copy(source.at[0, part], target.at[part], sems.at[i * chunks + j]))
            copies[-1].start()
    for i, (_, target, turned) in enumerate(sides):
        step = target.shape[0] // chunks
        for j in range(chunks):
            copies[i * chunks + j].wait()
            turned[:, j * step : (j + 1) * step] = target[j * step : (j + 1) * step].T


def slot_kernel(slots, x_size, first, second, own, tokens, cotangent, blocks, dispatch, combine):
    logits = first[...] + second[...]
    over_tokens, over_columns = softmax(logits, 1), softmax(logits, 0)
    dispatch[...] = over_tokens
    combine[...] = over_columns
    quarter = own.shape[2]
    core = lax.axis_index("core")
    for part, core in (((own[0], own[1]), core), ((tokens[...], cotangent[...]), 1 - core)):
        here = pl.ds(pl.multiple_of(core * quarter, quarter), quarter)
        slot_in = dot(over_tokens.astype(BF16), part[0], (1, 0))
        grad_out = dot(over_columns.astype(BF16), part[1], (1, 0))
        blocks[:, :, here] = to_blocks(slot_in, grad_out, slots, x_size)


def expert_kernel(slots, x_size, blocks, up_matrix, down_matrix, up_turned, down_turned, sums):
    got = blocks[...].astype(F32)
    first, second = jnp.split(got, x_size)
    in_order = lax.axis_index("x") != lax.axis_index("core")
    parts = (jnp.where(in_order, first, second), jnp.where(in_order, second, first))
    sides = [from_blocks(part, slots) for part in parts]
    forward, backward = (jnp.concatenate(side, axis=1).astype(BF16) for side in zip(*sides))
    preact = dot(forward, up_matrix[...], (1, 0))
    grad_hidden = dot(backward, down_turned[...], (1, 0))
    hidden, slope = gelu_parts(preact)
    sums[0] = dot(hidden.astype(BF16), down_matrix[...], (1, 0)).astype(BF16)
    sums[1] = dot((grad_hidden * slope).astype(BF16), up_turned[...], (1, 0)).astype(BF16)


def pair_kernel(slots, x_size, first, second, blocks):
    total = first[...].astype(F32) + second[...].astype(F32)
    blocks[...] = to_blocks(total[0], total[1], slots, x_size)


def image_kernel(
    slots, x_size, lead, middle, order, blocks, own, tokens, cotangent, across, corner, dispatch, combine, params, params_part, mixed, grad_tokens, rows
):
    half = lax.axis_index("x") * 2 + lax.axis_index("core")
    quarter = own.shape[2]
    slot_out, grad_in = from_blocks(sum(jnp.split(blocks[...].astype(F32), x_size)), slots)
    rows[0] = slot_out.astype(BF16)
    rows[1] = grad_in.astype(BF16)
    grad_combine = grad_dispatch = 0.0
    for offset, part in enumerate((own, (tokens, cotangent), across, corner)):
        start = pl.multiple_of(jnp.bitwise_xor(half, offset) * quarter, quarter)
        grad_combine += dot(rows[0, :, pl.ds(start, quarter)], part[1][...], (1, 1))
        grad_dispatch += dot(rows[1, :, pl.ds(start, quarter)], part[0][...], (1, 1))
    grad_logits = softmax_back(combine[...], grad_combine, 0) + softmax_back(dispatch[...], grad_dispatch, 1)
    partial = [dot(grad_logits.astype(BF16), part[0], (1, 0)) for part in (own, (tokens[...],))]
    partial = [outward(part, slots, lead).astype(BF16) for part in partial]
    early = lax.axis_index("expert") < middle
    sides = jnp.where(early, *partial), jnp.where(early, *partial[::-1])
    for i, image in enumerate(order):
        params_part[i] = sides[0 if image < middle else 1]
    here = pl.ds(pl.multiple_of(half * quarter, quarter), quarter)
    mixed[...] = dot(combine[...].astype(BF16), rows[0, :, here], (0, 0)).astype(BF16)
    token_term = dot(dispatch[...].astype(BF16), rows[1, :, here], (0, 0))
    grad_tokens[...] = (token_term + dot(grad_logits.astype(BF16), params[...], (0, 0))).astype(BF16)


def end_kernel(parts, mixed_here, grad_tokens_here, mixed, grad_tokens, grad_params):
    mixed[...] = mixed_here[...]
    grad_tokens[...] = grad_tokens_here[...]
    grad_params[...] = jnp.sum(parts[...].astype(F32), axis=0)


def call(kernel, outs, *args, scratch=(), in_hbm=(), limit=16):
    whole = pl.BlockSpec(memory_space=pltpu.VMEM)
    elsewhere = pl.BlockSpec(memory_space=pltpu.HBM)
    run = pl.pallas_call(
        kernel,
        out_shape=[jax.ShapeDtypeStruct(*out) if isinstance(out, tuple) else out for out in outs],
        in_specs=[elsewhere if i in in_hbm else whole for i in range(len(args))],
        out_specs=[whole] * len(outs),
        scratch_shapes=list(scratch),
        compiler_params=pltpu.CompilerParams(vmem_limit_bytes=limit * MIB),
    )
    return run(*(pltpu.with_memory_space_constraint(arg, pltpu.HBM) if i in in_hbm else arg for i, arg in enumerate(args)))


def local(experts, halves, tokens, slot_params, w_up, w_down, cotangent):
    seq, quarter = tokens.shape
    columns = slot_params.shape[1]
    slots = columns // experts
    x_size = halves // 2
    width = halves * quarter
    table = (columns, seq)
    lead, middle = experts * 5 // 8, experts // 2
    order = [(lead + i) % experts for i in range(experts)]
    wide = [
        [(expert * x_size + (x if core else 1 - x)) * 2 + core for core in (1, 0) for expert in order]
        for x in range(x_size)
    ]
    narrow = [
        [(image * x_size + x) * 2 + (side if image < middle else 1 - side) for image in order]
        for x in range(x_size)
        for side in (0, 1)
    ]
    axes = ("expert", "x", "core")

    beside = [swap(tokens, "core"), swap(cotangent, "core")]
    own, params, logits = call(
        functools.partial(start_kernel, slots, lead),
        [((2, seq, quarter), BF16), ((columns, quarter), BF16), (table, F32)],
        tokens,
        cotangent,
        slot_params.T,
        scratch=[pltpu.VMEM((columns, quarter), BF16), pltpu.SemaphoreType.DMA((3,))],
        in_hbm=(0, 1, 2),
    )
    (logits,) = call(
        functools.partial(add_kernel, slots, lead), [(table, F32)], logits, beside[0], swap(slot_params.T, "core")
    )
    other = swap(logits, "x")
    chunks = 2
    shapes = [w_up.shape[1:], w_down.shape[1:], w_up.shape[:0:-1], w_down.shape[:0:-1]]
    weights = call(
        functools.partial(weight_kernel, chunks),
        [pltpu.VMEM(shape, BF16) for shape in shapes],
        logits,
        w_up,
        w_down,
        scratch=[pltpu.SemaphoreType.DMA((2 * chunks,))],
        in_hbm=(1, 2),
    )
    other, own_later, *weights = lax.optimization_barrier((other, own, *weights))
    across = swap(own_later, "x")
    blocks, dispatch, combine = call(
        functools.partial(slot_kernel, slots, x_size),
        [((x_size * experts, 2 * slots, 2 * quarter), BF16), (table, F32), (table, F32)],
        logits,
        other,
        own,
        *beside,
    )

    blocks = lax.all_to_all(blocks, axes, 0, 0, tiled=True, axis_index_groups=wide)
    (sums,) = call(
        functools.partial(expert_kernel, slots, x_size), [((2, columns, width), BF16)], blocks, *weights
    )

    sums, across = lax.optimization_barrier((sums, across))
    other_sums = swap(sums, "core")
    corner = swap(across, "core")
    (blocks,) = call(
        functools.partial(pair_kernel, slots, x_size),
        [((x_size * experts, 2 * slots, width), BF16)],
        sums,
        other_sums,
    )
    blocks, corner = lax.optimization_barrier((blocks, corner))
    blocks = lax.all_to_all(blocks, axes, 0, 0, tiled=True, axis_index_groups=wide)
    params_part, mixed, grad_tokens = call(
        functools.partial(image_kernel, slots, x_size, lead, middle, order),
        [((experts, columns, quarter), BF16), pltpu.VMEM((seq, quarter), BF16), pltpu.VMEM((seq, quarter), BF16)],
        blocks,
        own,
        *beside,
        across,
        corner,
        dispatch,
        combine,
        params,
        scratch=[pltpu.VMEM((2, columns, width), BF16)],
        limit=16 if experts * columns <= 1024 else 48,
    )

    params_parts = lax.all_to_all(params_part, axes, 0, 0, tiled=True, axis_index_groups=narrow)
    mixed, grad_tokens, grad_params = call(
        end_kernel,
        [((seq, quarter), BF16), ((seq, quarter), BF16), ((columns, quarter), F32)],
        params_parts,
        mixed,
        grad_tokens,
        limit=16 if experts * columns <= 1024 else 48,
    )
    return mixed, grad_tokens, grad_params.T


def solution(mesh):
    experts, halves = mesh.shape["expert"], mesh.shape["half"]
    split = Mesh(mesh.devices.reshape(experts, halves // 2, 2), ("expert", "x", "core"))
    half = ("x", "core")
    in_specs = (
        P("expert", half),
        P(half, None),
        P("expert", None, half),
        P("expert", half, None),
        P("expert", half),
    )
    out_specs = (P("expert", half), P("expert", half), P(half, None))

    def program(*args):
        return jax.shard_map(
            lambda *blocks: local(experts, halves, *blocks),
            mesh=split,
            in_specs=in_specs,
            out_specs=out_specs,
            check_vma=False,
        )(*args)

    return program
```

```python
import functools

import jax
import jax.numpy as jnp
from jax import lax
from jax.experimental import pallas as pl
from jax.experimental.pallas import tpu as pltpu
from jax.sharding import Mesh, PartitionSpec as P

F32 = jnp.float32
BF16 = jnp.bfloat16
MIB = 2**20


def swap(array, axis):
    return lax.ppermute(array, axis, [(0, 1), (1, 0)])


def cross(array):
    return lax.ppermute(array, ("x", "core"), [(0, 3), (1, 2), (2, 1), (3, 0)])


def dot(left, right, over):
    return lax.dot_general(left, right, ((over[:1], over[1:]), ((), ())), preferred_element_type=F32)


def softmax(logits, axis):
    shifted = jnp.exp(logits - jnp.max(logits, axis=axis, keepdims=True))
    return shifted / jnp.sum(shifted, axis=axis, keepdims=True)


def softmax_back(probabilities, upstream, axis):
    inner = jnp.sum(probabilities * upstream, axis=axis, keepdims=True)
    return probabilities * (upstream - inner)


def gelu_parts(value):
    scale, cubic = 0.7978845608028654, 0.044715
    square = value * value
    curve = jnp.tanh(scale * (value + cubic * value * square))
    slope = 0.5 * (1.0 + curve) + 0.5 * value * (1.0 - curve * curve) * scale * (1.0 + 3.0 * cubic * square)
    return 0.5 * value * (1.0 + curve), slope


def inward(table, slots, lead):
    table = table.reshape(-1, slots, table.shape[1]).swapaxes(0, 1)
    table = jnp.concatenate([table[:, lead:], table[:, :lead]], axis=1)
    return table.reshape(-1, table.shape[2])


def outward(table, slots, lead):
    table = table.reshape(slots, -1, table.shape[1])
    lead = table.shape[1] - lead
    table = jnp.concatenate([table[:, lead:], table[:, :lead]], axis=1)
    return table.swapaxes(0, 1).reshape(-1, table.shape[2])


def to_blocks(forward, backward, slots, copies):
    rows = [part for table in (forward, backward) for part in jnp.split(table.astype(F32), slots)]
    blocks = jnp.stack(rows, axis=1).astype(BF16)
    return jnp.concatenate([blocks] * copies, axis=0)


def from_blocks(blocks, slots):
    rows = [blocks[:, i] for i in range(2 * slots)]
    return jnp.concatenate(rows[:slots], axis=0), jnp.concatenate(rows[slots:], axis=0)


def start_kernel(slots, lead, tokens, cotangent, params, own, params_in, logits, params_here, sems):
    copies = [
        pltpu.make_async_copy(source, target, sems.at[i])
        for i, (source, target) in enumerate(((params, params_here), (tokens, own.at[0]), (cotangent, own.at[1])))
    ]
    for copy in copies:
        copy.start()
    copies[0].wait()
    params_in[...] = inward(params_here[...].astype(F32), slots, lead).astype(BF16)
    copies[1].wait()
    logits[...] = dot(params_in[...], own[0], (1, 1))
    copies[2].wait()


def add_kernel(slots, lead, logits, tokens, params, total):
    params_in = inward(params[...].astype(F32), slots, lead).astype(BF16)
    total[...] = logits[...] + dot(params_in, tokens[...], (1, 1))


def weight_kernel(chunks, after, up_matrix, down_matrix, up_here, down_here, up_turned, down_turned, sems):
    sides = ((up_matrix, up_here, up_turned), (down_matrix, down_here, down_turned))
    copies = []
    for i, (source, target, _) in enumerate(sides):
        step = source.shape[1] // chunks
        for j in range(chunks):
            part = pl.ds(j * step, step)
            copies.append(pltpu.make_async_copy(source.at[0, part], target.at[part], sems.at[i * chunks + j]))
            copies[-1].start()
    for i, (_, target, turned) in enumerate(sides):
        step = target.shape[0] // chunks
        for j in range(chunks):
            copies[i * chunks + j].wait()
            turned[:, j * step : (j + 1) * step] = target[j * step : (j + 1) * step].T


def slot_kernel(slots, x_size, first, second, own, tokens, cotangent, blocks, dispatch, combine):
    logits = first[...] + second[...]
    over_tokens, over_columns = softmax(logits, 1), softmax(logits, 0)
    dispatch[...] = over_tokens
    combine[...] = over_columns
    quarter = own.shape[2]
    core = lax.axis_index("core")
    for part, core in (((own[0], own[1]), core), ((tokens[...], cotangent[...]), 1 - core)):
        here = pl.ds(pl.multiple_of(core * quarter, quarter), quarter)
        slot_in = dot(over_tokens.astype(BF16), part[0], (1, 0))
        grad_out = dot(over_columns.astype(BF16), part[1], (1, 0))
        blocks[:, :, here] = to_blocks(slot_in, grad_out, slots, x_size)


def expert_kernel(slots, x_size, blocks, up_matrix, down_matrix, up_turned, down_turned, sums):
    got = blocks[...].astype(F32)
    first, second = jnp.split(got, x_size)
    in_order = lax.axis_index("x") != lax.axis_index("core")
    parts = (jnp.where(in_order, first, second), jnp.where(in_order, second, first))
    sides = [from_blocks(part, slots) for part in parts]
    forward, backward = (jnp.concatenate(side, axis=1).astype(BF16) for side in zip(*sides))
    preact = dot(forward, up_matrix[...], (1, 0))
    grad_hidden = dot(backward, down_turned[...], (1, 0))
    hidden, slope = gelu_parts(preact)
    sums[0] = dot(hidden.astype(BF16), down_matrix[...], (1, 0)).astype(BF16)
    sums[1] = dot((grad_hidden * slope).astype(BF16), up_turned[...], (1, 0)).astype(BF16)


def pair_kernel(slots, x_size, first, second, blocks):
    total = first[...].astype(F32) + second[...].astype(F32)
    blocks[...] = to_blocks(total[0], total[1], slots, x_size)


def image_kernel(
    slots, x_size, lead, middle, order, blocks, own, tokens, cotangent, across, corner, dispatch, combine, params, params_part, mixed, grad_tokens, rows
):
    half = lax.axis_index("x") * 2 + lax.axis_index("core")
    quarter = own.shape[2]
    slot_out, grad_in = from_blocks(sum(jnp.split(blocks[...].astype(F32), x_size)), slots)
    rows[0] = slot_out.astype(BF16)
    rows[1] = grad_in.astype(BF16)
    grad_combine = grad_dispatch = 0.0
    for offset, part in enumerate((own, (tokens, cotangent), corner, across)):
        start = pl.multiple_of(jnp.bitwise_xor(half, offset) * quarter, quarter)
        grad_combine += dot(rows[0, :, pl.ds(start, quarter)], part[1][...], (1, 1))
        grad_dispatch += dot(rows[1, :, pl.ds(start, quarter)], part[0][...], (1, 1))
    grad_logits = softmax_back(combine[...], grad_combine, 0) + softmax_back(dispatch[...], grad_dispatch, 1)
    partial = [dot(grad_logits.astype(BF16), part[0], (1, 0)) for part in (own, (tokens[...],))]
    partial = [outward(part, slots, lead).astype(BF16) for part in partial]
    early = lax.axis_index("expert") < middle
    sides = jnp.where(early, *partial), jnp.where(early, *partial[::-1])
    for i, image in enumerate(order):
        params_part[i] = sides[0 if image < middle else 1]
    here = pl.ds(pl.multiple_of(half * quarter, quarter), quarter)
    mixed[...] = dot(combine[...].astype(BF16), rows[0, :, here], (0, 0)).astype(BF16)
    token_term = dot(dispatch[...].astype(BF16), rows[1, :, here], (0, 0))
    grad_tokens[...] = (token_term + dot(grad_logits.astype(BF16), params[...], (0, 0))).astype(BF16)


def end_kernel(parts, mixed_here, grad_tokens_here, mixed, grad_tokens, grad_params):
    mixed[...] = mixed_here[...]
    grad_tokens[...] = grad_tokens_here[...]
    grad_params[...] = jnp.sum(parts[...].astype(F32), axis=0)


def call(kernel, outs, *args, scratch=(), in_hbm=(), limit=16):
    whole = pl.BlockSpec(memory_space=pltpu.VMEM)
    elsewhere = pl.BlockSpec(memory_space=pltpu.HBM)
    run = pl.pallas_call(
        kernel,
        out_shape=[jax.ShapeDtypeStruct(*out) if isinstance(out, tuple) else out for out in outs],
        in_specs=[elsewhere if i in in_hbm else whole for i in range(len(args))],
        out_specs=[whole] * len(outs),
        scratch_shapes=list(scratch),
        compiler_params=pltpu.CompilerParams(vmem_limit_bytes=limit * MIB),
    )
    return run(*(pltpu.with_memory_space_constraint(arg, pltpu.HBM) if i in in_hbm else arg for i, arg in enumerate(args)))


def local(experts, halves, tokens, slot_params, w_up, w_down, cotangent):
    seq, quarter = tokens.shape
    columns = slot_params.shape[1]
    slots = columns // experts
    x_size = halves // 2
    width = halves * quarter
    table = (columns, seq)
    lead, middle = experts * 5 // 8, experts // 2
    order = [(lead + i) % experts for i in range(experts)]
    wide = [
        [(expert * x_size + (x if core else 1 - x)) * 2 + core for core in (1, 0) for expert in order]
        for x in range(x_size)
    ]
    narrow = [
        [(image * x_size + x) * 2 + (side if image < middle else 1 - side) for image in order]
        for x in range(x_size)
        for side in (0, 1)
    ]
    axes = ("expert", "x", "core")

    beside = [swap(tokens, "core"), swap(cotangent, "core")]
    own, params, logits = call(
        functools.partial(start_kernel, slots, lead),
        [((2, seq, quarter), BF16), ((columns, quarter), BF16), (table, F32)],
        tokens,
        cotangent,
        slot_params.T,
        scratch=[pltpu.VMEM((columns, quarter), BF16), pltpu.SemaphoreType.DMA((3,))],
        in_hbm=(0, 1, 2),
    )
    (logits,) = call(
        functools.partial(add_kernel, slots, lead), [(table, F32)], logits, beside[0], swap(slot_params.T, "core")
    )
    other = cross(logits)
    chunks = 2
    shapes = [w_up.shape[1:], w_down.shape[1:], w_up.shape[:0:-1], w_down.shape[:0:-1]]
    weights = call(
        functools.partial(weight_kernel, chunks),
        [pltpu.VMEM(shape, BF16) for shape in shapes],
        logits,
        w_up,
        w_down,
        scratch=[pltpu.SemaphoreType.DMA((2 * chunks,))],
        in_hbm=(1, 2),
    )
    other, own_later, *weights = lax.optimization_barrier((other, own, *weights))
    across = cross(own_later)
    blocks, dispatch, combine = call(
        functools.partial(slot_kernel, slots, x_size),
        [((x_size * experts, 2 * slots, 2 * quarter), BF16), (table, F32), (table, F32)],
        logits,
        other,
        own,
        *beside,
    )

    blocks = lax.all_to_all(blocks, axes, 0, 0, tiled=True, axis_index_groups=wide)
    (sums,) = call(
        functools.partial(expert_kernel, slots, x_size), [((2, columns, width), BF16)], blocks, *weights
    )

    sums, across = lax.optimization_barrier((sums, across))
    other_sums = swap(sums, "core")
    corner = swap(across, "core")
    (blocks,) = call(
        functools.partial(pair_kernel, slots, x_size),
        [((x_size * experts, 2 * slots, width), BF16)],
        sums,
        other_sums,
    )
    blocks, corner = lax.optimization_barrier((blocks, corner))
    blocks = lax.all_to_all(blocks, axes, 0, 0, tiled=True, axis_index_groups=wide)
    params_part, mixed, grad_tokens = call(
        functools.partial(image_kernel, slots, x_size, lead, middle, order),
        [((experts, columns, quarter), BF16), pltpu.VMEM((seq, quarter), BF16), pltpu.VMEM((seq, quarter), BF16)],
        blocks,
        own,
        *beside,
        across,
        corner,
        dispatch,
        combine,
        params,
        scratch=[pltpu.VMEM((2, columns, width), BF16)],
        limit=16 if experts * columns <= 1024 else 48,
    )

    params_parts = lax.all_to_all(params_part, axes, 0, 0, tiled=True, axis_index_groups=narrow)
    mixed, grad_tokens, grad_params = call(
        end_kernel,
        [((seq, quarter), BF16), ((seq, quarter), BF16), ((columns, quarter), F32)],
        params_parts,
        mixed,
        grad_tokens,
        limit=16 if experts * columns <= 1024 else 48,
    )
    return mixed, grad_tokens, grad_params.T


def solution(mesh):
    experts, halves = mesh.shape["expert"], mesh.shape["half"]
    split = Mesh(mesh.devices.reshape(experts, halves // 2, 2), ("expert", "x", "core"))
    half = ("x", "core")
    in_specs = (
        P("expert", half),
        P(half, None),
        P("expert", None, half),
        P("expert", half, None),
        P("expert", half),
    )
    out_specs = (P("expert", half), P("expert", half), P(half, None))

    def program(*args):
        return jax.shard_map(
            lambda *blocks: local(experts, halves, *blocks),
            mesh=split,
            in_specs=in_specs,
            out_specs=out_specs,
            check_vma=False,
        )(*args)

    return program
```

```python
import functools

import jax
import jax.numpy as jnp
from jax import lax
from jax.experimental import pallas as pl
from jax.experimental.pallas import tpu as pltpu
from jax.sharding import Mesh, PartitionSpec as P

F32 = jnp.float32
BF16 = jnp.bfloat16
MIB = 2**20


def swap(array, axis):
    return lax.ppermute(array, axis, [(0, 1), (1, 0)])


def cross(array):
    return lax.ppermute(array, ("x", "core"), [(0, 3), (1, 2), (2, 1), (3, 0)])


def dot(left, right, over):
    return lax.dot_general(left, right, ((over[:1], over[1:]), ((), ())), preferred_element_type=F32)


def softmax(logits, axis):
    shifted = jnp.exp(logits - jnp.max(logits, axis=axis, keepdims=True))
    return shifted / jnp.sum(shifted, axis=axis, keepdims=True)


def softmax_back(probabilities, upstream, axis):
    inner = jnp.sum(probabilities * upstream, axis=axis, keepdims=True)
    return probabilities * (upstream - inner)


def gelu_parts(value):
    scale, cubic = 0.7978845608028654, 0.044715
    square = value * value
    curve = jnp.tanh(scale * (value + cubic * value * square))
    slope = 0.5 * (1.0 + curve) + 0.5 * value * (1.0 - curve * curve) * scale * (1.0 + 3.0 * cubic * square)
    return 0.5 * value * (1.0 + curve), slope


def inward(table, slots, lead):
    table = table.reshape(-1, slots, table.shape[1]).swapaxes(0, 1)
    table = jnp.concatenate([table[:, lead:], table[:, :lead]], axis=1)
    return table.reshape(-1, table.shape[2])


def outward(table, slots, lead):
    table = table.reshape(slots, -1, table.shape[1])
    lead = table.shape[1] - lead
    table = jnp.concatenate([table[:, lead:], table[:, :lead]], axis=1)
    return table.swapaxes(0, 1).reshape(-1, table.shape[2])


def to_blocks(forward, backward, slots, copies):
    rows = [part for table in (forward, backward) for part in jnp.split(table.astype(F32), slots)]
    blocks = jnp.stack(rows, axis=1).astype(BF16)
    return jnp.concatenate([blocks] * copies, axis=0)


def from_blocks(blocks, slots):
    rows = [blocks[:, i] for i in range(2 * slots)]
    return jnp.concatenate(rows[:slots], axis=0), jnp.concatenate(rows[slots:], axis=0)


def start_kernel(slots, lead, tokens, cotangent, params, own, params_in, logits, params_here, sems):
    copies = [
        pltpu.make_async_copy(source, target, sems.at[i])
        for i, (source, target) in enumerate(((params, params_here), (tokens, own.at[0]), (cotangent, own.at[1])))
    ]
    for copy in copies:
        copy.start()
    copies[0].wait()
    params_in[...] = inward(params_here[...].astype(F32), slots, lead).astype(BF16)
    copies[1].wait()
    logits[...] = dot(params_in[...], own[0], (1, 1))
    copies[2].wait()


def add_kernel(slots, lead, logits, tokens, params, total):
    params_in = inward(params[...].astype(F32), slots, lead).astype(BF16)
    total[...] = logits[...] + dot(params_in, tokens[...], (1, 1))


def weight_kernel(chunks, after, up_matrix, down_matrix, up_here, down_here, up_turned, down_turned, sems):
    sides = ((up_matrix, up_here, up_turned), (down_matrix, down_here, down_turned))
    copies = []
    for i, (source, target, _) in enumerate(sides):
        step = source.shape[1] // chunks
        for j in range(chunks):
            part = pl.ds(j * step, step)
            copies.append(pltpu.make_async_copy(source.at[0, part], target.at[part], sems.at[i * chunks + j]))
            copies[-1].start()
    for i, (_, target, turned) in enumerate(sides):
        step = target.shape[0] // chunks
        for j in range(chunks):
            copies[i * chunks + j].wait()
            turned[:, j * step : (j + 1) * step] = target[j * step : (j + 1) * step].T


def slot_kernel(slots, x_size, first, second, own, tokens, cotangent, blocks, dispatch, combine):
    logits = first[...] + second[...]
    over_tokens, over_columns = softmax(logits, 1), softmax(logits, 0)
    dispatch[...] = over_tokens
    combine[...] = over_columns
    quarter = own.shape[2]
    core = lax.axis_index("core")
    for part, core in (((own[0], own[1]), core), ((tokens[...], cotangent[...]), 1 - core)):
        here = pl.ds(pl.multiple_of(core * quarter, quarter), quarter)
        slot_in = dot(over_tokens.astype(BF16), part[0], (1, 0))
        grad_out = dot(over_columns.astype(BF16), part[1], (1, 0))
        blocks[:, :, here] = to_blocks(slot_in, grad_out, slots, x_size)


def expert_kernel(slots, x_size, blocks, up_matrix, down_matrix, up_turned, down_turned, sums):
    got = blocks[...].astype(F32)
    first, second = jnp.split(got, x_size)
    in_order = lax.axis_index("x") != lax.axis_index("core")
    parts = (jnp.where(in_order, first, second), jnp.where(in_order, second, first))
    sides = [from_blocks(part, slots) for part in parts]
    forward, backward = (jnp.concatenate(side, axis=1).astype(BF16) for side in zip(*sides))
    preact = dot(forward, up_matrix[...], (1, 0))
    grad_hidden = dot(backward, down_turned[...], (1, 0))
    hidden, slope = gelu_parts(preact)
    sums[0] = dot(hidden.astype(BF16), down_matrix[...], (1, 0)).astype(BF16)
    sums[1] = dot((grad_hidden * slope).astype(BF16), up_turned[...], (1, 0)).astype(BF16)


def pair_kernel(slots, x_size, first, second, blocks):
    total = first[...].astype(F32) + second[...].astype(F32)
    blocks[...] = to_blocks(total[0], total[1], slots, x_size)


def image_kernel(
    slots, x_size, lead, middle, order, blocks, own, tokens, cotangent, across, corner, dispatch, combine, params, params_part, mixed, grad_tokens, rows
):
    half = lax.axis_index("x") * 2 + lax.axis_index("core")
    quarter = own.shape[2]
    slot_out, grad_in = from_blocks(sum(jnp.split(blocks[...].astype(F32), x_size)), slots)
    rows[0] = slot_out.astype(BF16)
    rows[1] = grad_in.astype(BF16)
    grad_combine = grad_dispatch = 0.0
    for offset, part in enumerate((own, (tokens, cotangent), corner, across)):
        start = pl.multiple_of(jnp.bitwise_xor(half, offset) * quarter, quarter)
        grad_combine += dot(rows[0, :, pl.ds(start, quarter)], part[1][...], (1, 1))
        grad_dispatch += dot(rows[1, :, pl.ds(start, quarter)], part[0][...], (1, 1))
    grad_logits = softmax_back(combine[...], grad_combine, 0) + softmax_back(dispatch[...], grad_dispatch, 1)
    partial = [dot(grad_logits.astype(BF16), part[0], (1, 0)) for part in (own, (tokens[...],))]
    partial = [outward(part, slots, lead).astype(BF16) for part in partial]
    early = lax.axis_index("expert") < middle
    sides = jnp.where(early, *partial), jnp.where(early, *partial[::-1])
    for i, image in enumerate(order):
        params_part[i] = sides[0 if image < middle else 1]
    here = pl.ds(pl.multiple_of(half * quarter, quarter), quarter)
    mixed[...] = dot(combine[...].astype(BF16), rows[0, :, here], (0, 0)).astype(BF16)
    token_term = dot(dispatch[...].astype(BF16), rows[1, :, here], (0, 0))
    grad_tokens[...] = (token_term + dot(grad_logits.astype(BF16), params[...], (0, 0))).astype(BF16)


def end_kernel(parts, mixed_here, grad_tokens_here, mixed, grad_tokens, grad_params):
    mixed[...] = mixed_here[...]
    grad_tokens[...] = grad_tokens_here[...]
    grad_params[...] = jnp.sum(parts[...].astype(F32), axis=0)


def call(kernel, outs, *args, scratch=(), in_hbm=(), limit=16):
    whole = pl.BlockSpec(memory_space=pltpu.VMEM)
    elsewhere = pl.BlockSpec(memory_space=pltpu.HBM)
    run = pl.pallas_call(
        kernel,
        out_shape=[jax.ShapeDtypeStruct(*out) if isinstance(out, tuple) else out for out in outs],
        in_specs=[elsewhere if i in in_hbm else whole for i in range(len(args))],
        out_specs=[whole] * len(outs),
        scratch_shapes=list(scratch),
        compiler_params=pltpu.CompilerParams(vmem_limit_bytes=limit * MIB),
    )
    return run(*(pltpu.with_memory_space_constraint(arg, pltpu.HBM) if i in in_hbm else arg for i, arg in enumerate(args)))


def local(experts, halves, tokens, slot_params, w_up, w_down, cotangent):
    seq, quarter = tokens.shape
    columns = slot_params.shape[1]
    slots = columns // experts
    x_size = halves // 2
    width = halves * quarter
    table = (columns, seq)
    lead, middle = experts * 5 // 8, experts // 2
    order = [(lead + i) % experts for i in range(experts)]
    near = [lead] + [i for i in range(experts) if i != lead]
    wide = [
        [(expert * x_size + (x if core else 1 - x)) * 2 + core for core in (1, 0) for expert in order]
        for x in range(x_size)
    ]
    narrow = [
        [(image * x_size + x) * 2 + (side if image < middle else 1 - side) for image in near]
        for x in range(x_size)
        for side in (0, 1)
    ]
    axes = ("expert", "x", "core")

    beside = [swap(tokens, "core"), swap(cotangent, "core")]
    own, params, logits = call(
        functools.partial(start_kernel, slots, lead),
        [((2, seq, quarter), BF16), ((columns, quarter), BF16), (table, F32)],
        tokens,
        cotangent,
        slot_params.T,
        scratch=[pltpu.VMEM((columns, quarter), BF16), pltpu.SemaphoreType.DMA((3,))],
        in_hbm=(0, 1, 2),
    )
    (logits,) = call(
        functools.partial(add_kernel, slots, lead), [(table, F32)], logits, beside[0], swap(slot_params.T, "core")
    )
    other = cross(logits)
    chunks = 2
    shapes = [w_up.shape[1:], w_down.shape[1:], w_up.shape[:0:-1], w_down.shape[:0:-1]]
    weights = call(
        functools.partial(weight_kernel, chunks),
        [pltpu.VMEM(shape, BF16) for shape in shapes],
        logits,
        w_up,
        w_down,
        scratch=[pltpu.SemaphoreType.DMA((2 * chunks,))],
        in_hbm=(1, 2),
    )
    other, own_later, *weights = lax.optimization_barrier((other, own, *weights))
    across = cross(own_later)
    blocks, dispatch, combine = call(
        functools.partial(slot_kernel, slots, x_size),
        [((x_size * experts, 2 * slots, 2 * quarter), BF16), (table, F32), (table, F32)],
        logits,
        other,
        own,
        *beside,
    )

    blocks = lax.all_to_all(blocks, axes, 0, 0, tiled=True, axis_index_groups=wide)
    (sums,) = call(
        functools.partial(expert_kernel, slots, x_size), [((2, columns, width), BF16)], blocks, *weights
    )

    sums, across = lax.optimization_barrier((sums, across))
    other_sums = swap(sums, "core")
    corner = swap(across, "core")
    (blocks,) = call(
        functools.partial(pair_kernel, slots, x_size),
        [((x_size * experts, 2 * slots, width), BF16)],
        sums,
        other_sums,
    )
    blocks, corner = lax.optimization_barrier((blocks, corner))
    blocks = lax.all_to_all(blocks, axes, 0, 0, tiled=True, axis_index_groups=wide)
    params_part, mixed, grad_tokens = call(
        functools.partial(image_kernel, slots, x_size, lead, middle, near),
        [((experts, columns, quarter), BF16), pltpu.VMEM((seq, quarter), BF16), pltpu.VMEM((seq, quarter), BF16)],
        blocks,
        own,
        *beside,
        across,
        corner,
        dispatch,
        combine,
        params,
        scratch=[pltpu.VMEM((2, columns, width), BF16)],
        limit=16 if experts * columns <= 1024 else 48,
    )

    params_parts = lax.all_to_all(params_part, axes, 0, 0, tiled=True, axis_index_groups=narrow)
    mixed, grad_tokens, grad_params = call(
        end_kernel,
        [((seq, quarter), BF16), ((seq, quarter), BF16), ((columns, quarter), F32)],
        params_parts,
        mixed,
        grad_tokens,
        limit=16 if experts * columns <= 1024 else 48,
    )
    return mixed, grad_tokens, grad_params.T


def solution(mesh):
    experts, halves = mesh.shape["expert"], mesh.shape["half"]
    split = Mesh(mesh.devices.reshape(experts, halves // 2, 2), ("expert", "x", "core"))
    half = ("x", "core")
    in_specs = (
        P("expert", half),
        P(half, None),
        P("expert", None, half),
        P("expert", half, None),
        P("expert", half),
    )
    out_specs = (P("expert", half), P("expert", half), P(half, None))

    def program(*args):
        return jax.shard_map(
            lambda *blocks: local(experts, halves, *blocks),
            mesh=split,
            in_specs=in_specs,
            out_specs=out_specs,
            check_vma=False,
        )(*args)

    return program
```

```python
import functools

import jax
import jax.numpy as jnp
from jax import lax
from jax.experimental import pallas as pl
from jax.experimental.pallas import tpu as pltpu
from jax.sharding import Mesh, PartitionSpec as P

F32 = jnp.float32
BF16 = jnp.bfloat16
MIB = 2**20


def swap(array, axis):
    return lax.ppermute(array, axis, [(0, 1), (1, 0)])


def cross(array, halves):
    return lax.ppermute(array, ("x", "core"), [(i, halves - 1 - i) for i in range(halves)])


def dot(left, right, over):
    return lax.dot_general(left, right, ((over[:1], over[1:]), ((), ())), preferred_element_type=F32)


def softmax(logits, axis):
    shifted = jnp.exp(logits - jnp.max(logits, axis=axis, keepdims=True))
    return shifted / jnp.sum(shifted, axis=axis, keepdims=True)


def softmax_back(probabilities, upstream, axis):
    inner = jnp.sum(probabilities * upstream, axis=axis, keepdims=True)
    return probabilities * (upstream - inner)


def gelu_parts(value):
    scale, cubic = 0.7978845608028654, 0.044715
    square = value * value
    curve = jnp.tanh(scale * (value + cubic * value * square))
    slope = 0.5 * (1.0 + curve) + 0.5 * value * (1.0 - curve * curve) * scale * (1.0 + 3.0 * cubic * square)
    return 0.5 * value * (1.0 + curve), slope


def inward(table, slots, lead):
    table = table.reshape(-1, slots, table.shape[1]).swapaxes(0, 1)
    table = jnp.concatenate([table[:, lead:], table[:, :lead]], axis=1)
    return table.reshape(-1, table.shape[2])


def outward(table, slots, lead):
    table = table.reshape(slots, -1, table.shape[1])
    lead = table.shape[1] - lead
    table = jnp.concatenate([table[:, lead:], table[:, :lead]], axis=1)
    return table.swapaxes(0, 1).reshape(-1, table.shape[2])


def to_blocks(forward, backward, slots, copies):
    rows = [part for table in (forward, backward) for part in jnp.split(table.astype(F32), slots)]
    blocks = jnp.stack(rows, axis=1).astype(BF16)
    return jnp.concatenate([blocks] * copies, axis=0)


def from_blocks(blocks, slots):
    rows = [blocks[:, i] for i in range(2 * slots)]
    return jnp.concatenate(rows[:slots], axis=0), jnp.concatenate(rows[slots:], axis=0)


def start_kernel(slots, lead, tokens, cotangent, params, own, params_in, logits, params_here, sems):
    copies = [
        pltpu.make_async_copy(source, target, sems.at[i])
        for i, (source, target) in enumerate(((params, params_here), (tokens, own.at[0]), (cotangent, own.at[1])))
    ]
    for copy in copies:
        copy.start()
    copies[0].wait()
    params_in[...] = inward(params_here[...].astype(F32), slots, lead).astype(BF16)
    copies[1].wait()
    logits[...] = dot(params_in[...], own[0], (1, 1))
    copies[2].wait()


def add_kernel(slots, lead, logits, tokens, params, total):
    params_in = inward(params[...].astype(F32), slots, lead).astype(BF16)
    total[...] = logits[...] + dot(params_in, tokens[...], (1, 1))


def weight_kernel(chunks, after, up_matrix, down_matrix, up_here, down_here, up_turned, down_turned, sems):
    sides = ((up_matrix, up_here, up_turned), (down_matrix, down_here, down_turned))
    copies = []
    for i, (source, target, _) in enumerate(sides):
        step = source.shape[1] // chunks
        for j in range(chunks):
            part = pl.ds(j * step, step)
            copies.append(pltpu.make_async_copy(source.at[0, part], target.at[part], sems.at[i * chunks + j]))
            copies[-1].start()
    for i, (_, target, turned) in enumerate(sides):
        step = target.shape[0] // chunks
        for j in range(chunks):
            copies[i * chunks + j].wait()
            turned[:, j * step : (j + 1) * step] = target[j * step : (j + 1) * step].T


def slot_kernel(slots, x_size, first, second, own, tokens, cotangent, blocks, dispatch, combine):
    logits = first[...] + second[...]
    over_tokens, over_columns = softmax(logits, 1), softmax(logits, 0)
    dispatch[...] = over_tokens
    combine[...] = over_columns
    quarter = own.shape[2]
    core = lax.axis_index("core")
    for part, core in (((own[0], own[1]), core), ((tokens[...], cotangent[...]), 1 - core)):
        here = pl.ds(pl.multiple_of(core * quarter, quarter), quarter)
        slot_in = dot(over_tokens.astype(BF16), part[0], (1, 0))
        grad_out = dot(over_columns.astype(BF16), part[1], (1, 0))
        blocks[:, :, here] = to_blocks(slot_in, grad_out, slots, x_size)


def expert_kernel(slots, x_size, blocks, up_matrix, down_matrix, up_turned, down_turned, sums):
    got = blocks[...].astype(F32)
    first, second = jnp.split(got, x_size)
    in_order = lax.axis_index("x") != lax.axis_index("core")
    parts = (jnp.where(in_order, first, second), jnp.where(in_order, second, first))
    sides = [from_blocks(part, slots) for part in parts]
    forward, backward = (jnp.concatenate(side, axis=1).astype(BF16) for side in zip(*sides))
    preact = dot(forward, up_matrix[...], (1, 0))
    grad_hidden = dot(backward, down_turned[...], (1, 0))
    hidden, slope = gelu_parts(preact)
    sums[0] = dot(hidden.astype(BF16), down_matrix[...], (1, 0)).astype(BF16)
    sums[1] = dot((grad_hidden * slope).astype(BF16), up_turned[...], (1, 0)).astype(BF16)


def pair_kernel(slots, x_size, first, second, blocks):
    total = first[...].astype(F32) + second[...].astype(F32)
    blocks[...] = to_blocks(total[0], total[1], slots, x_size)


def image_kernel(
    slots, x_size, lead, middle, order, blocks, own, tokens, cotangent, across, corner, dispatch, combine, params, params_part, mixed, grad_tokens, rows
):
    half = lax.axis_index("x") * 2 + lax.axis_index("core")
    quarter = own.shape[2]
    slot_out, grad_in = from_blocks(sum(jnp.split(blocks[...].astype(F32), x_size)), slots)
    rows[0] = slot_out.astype(BF16)
    rows[1] = grad_in.astype(BF16)
    grad_combine = grad_dispatch = 0.0
    for offset, part in enumerate((own, (tokens, cotangent), corner, across)):
        start = pl.multiple_of(jnp.bitwise_xor(half, offset) * quarter, quarter)
        grad_combine += dot(rows[0, :, pl.ds(start, quarter)], part[1][...], (1, 1))
        grad_dispatch += dot(rows[1, :, pl.ds(start, quarter)], part[0][...], (1, 1))
    grad_logits = softmax_back(combine[...], grad_combine, 0) + softmax_back(dispatch[...], grad_dispatch, 1)
    partial = [dot(grad_logits.astype(BF16), part[0], (1, 0)) for part in (own, (tokens[...],))]
    partial = [outward(part, slots, lead).astype(BF16) for part in partial]
    early = lax.axis_index("expert") < middle
    sides = jnp.where(early, *partial), jnp.where(early, *partial[::-1])
    for i, image in enumerate(order):
        params_part[i] = sides[0 if image < middle else 1]
    here = pl.ds(pl.multiple_of(half * quarter, quarter), quarter)
    mixed[...] = dot(combine[...].astype(BF16), rows[0, :, here], (0, 0)).astype(BF16)
    token_term = dot(dispatch[...].astype(BF16), rows[1, :, here], (0, 0))
    grad_tokens[...] = (token_term + dot(grad_logits.astype(BF16), params[...], (0, 0))).astype(BF16)


def end_kernel(parts, mixed_here, grad_tokens_here, mixed, grad_tokens, grad_params):
    mixed[...] = mixed_here[...]
    grad_tokens[...] = grad_tokens_here[...]
    grad_params[...] = jnp.sum(parts[...].astype(F32), axis=0)


def call(kernel, outs, *args, scratch=(), in_hbm=(), limit=16):
    whole = pl.BlockSpec(memory_space=pltpu.VMEM)
    elsewhere = pl.BlockSpec(memory_space=pltpu.HBM)
    run = pl.pallas_call(
        kernel,
        out_shape=[jax.ShapeDtypeStruct(*out) if isinstance(out, tuple) else out for out in outs],
        in_specs=[elsewhere if i in in_hbm else whole for i in range(len(args))],
        out_specs=[whole] * len(outs),
        scratch_shapes=list(scratch),
        compiler_params=pltpu.CompilerParams(vmem_limit_bytes=limit * MIB),
    )
    return run(*(pltpu.with_memory_space_constraint(arg, pltpu.HBM) if i in in_hbm else arg for i, arg in enumerate(args)))


def local(experts, halves, tokens, slot_params, w_up, w_down, cotangent):
    seq, quarter = tokens.shape
    columns = slot_params.shape[1]
    slots = columns // experts
    x_size = halves // 2
    width = halves * quarter
    table = (columns, seq)
    lead, middle = experts * 5 // 8, experts // 2
    order = [(lead + i) % experts for i in range(experts)]
    near = [lead] + [i for i in range(experts) if i != lead]
    wide = [
        [(expert * x_size + (x if core else 1 - x)) * 2 + core for core in (1, 0) for expert in order]
        for x in range(x_size)
    ]
    narrow = [
        [(image * x_size + x) * 2 + (side if image < middle else 1 - side) for image in near]
        for x in range(x_size)
        for side in (0, 1)
    ]
    axes = ("expert", "x", "core")

    beside = [swap(tokens, "core"), swap(cotangent, "core")]
    own, params, logits = call(
        functools.partial(start_kernel, slots, lead),
        [((2, seq, quarter), BF16), ((columns, quarter), BF16), (table, F32)],
        tokens,
        cotangent,
        slot_params.T,
        scratch=[pltpu.VMEM((columns, quarter), BF16), pltpu.SemaphoreType.DMA((3,))],
        in_hbm=(0, 1, 2),
    )
    (logits,) = call(
        functools.partial(add_kernel, slots, lead), [(table, F32)], logits, beside[0], swap(slot_params.T, "core")
    )
    other = cross(logits, halves)
    chunks = 2
    shapes = [w_up.shape[1:], w_down.shape[1:], w_up.shape[:0:-1], w_down.shape[:0:-1]]
    weights = call(
        functools.partial(weight_kernel, chunks),
        [pltpu.VMEM(shape, BF16) for shape in shapes],
        logits,
        w_up,
        w_down,
        scratch=[pltpu.SemaphoreType.DMA((2 * chunks,))],
        in_hbm=(1, 2),
    )
    other, own_later, *weights = lax.optimization_barrier((other, own, *weights))
    across = cross(own_later, halves)
    blocks, dispatch, combine = call(
        functools.partial(slot_kernel, slots, x_size),
        [((x_size * experts, 2 * slots, 2 * quarter), BF16), (table, F32), (table, F32)],
        logits,
        other,
        own,
        *beside,
    )

    blocks = lax.all_to_all(blocks, axes, 0, 0, tiled=True, axis_index_groups=wide)
    (sums,) = call(
        functools.partial(expert_kernel, slots, x_size), [((2, columns, width), BF16)], blocks, *weights
    )

    sums, across = lax.optimization_barrier((sums, across))
    other_sums = swap(sums, "core")
    corner = swap(across, "core")
    (blocks,) = call(
        functools.partial(pair_kernel, slots, x_size),
        [((x_size * experts, 2 * slots, width), BF16)],
        sums,
        other_sums,
    )
    blocks, corner = lax.optimization_barrier((blocks, corner))
    blocks = lax.all_to_all(blocks, axes, 0, 0, tiled=True, axis_index_groups=wide)
    params_part, mixed, grad_tokens = call(
        functools.partial(image_kernel, slots, x_size, lead, middle, near),
        [((experts, columns, quarter), BF16), pltpu.VMEM((seq, quarter), BF16), pltpu.VMEM((seq, quarter), BF16)],
        blocks,
        own,
        *beside,
        across,
        corner,
        dispatch,
        combine,
        params,
        scratch=[pltpu.VMEM((2, columns, width), BF16)],
        limit=16 if experts * columns <= 1024 else 48,
    )

    params_parts = lax.all_to_all(params_part, axes, 0, 0, tiled=True, axis_index_groups=narrow)
    mixed, grad_tokens, grad_params = call(
        end_kernel,
        [((seq, quarter), BF16), ((seq, quarter), BF16), ((columns, quarter), F32)],
        params_parts,
        mixed,
        grad_tokens,
        limit=16 if experts * columns <= 1024 else 48,
    )
    return mixed, grad_tokens, grad_params.T


def solution(mesh):
    experts, halves = mesh.shape["expert"], mesh.shape["half"]
    split = Mesh(mesh.devices.reshape(experts, halves // 2, 2), ("expert", "x", "core"))
    half = ("x", "core")
    in_specs = (
        P("expert", half),
        P(half, None),
        P("expert", None, half),
        P("expert", half, None),
        P("expert", half),
    )
    out_specs = (P("expert", half), P("expert", half), P(half, None))

    def program(*args):
        return jax.shard_map(
            lambda *blocks: local(experts, halves, *blocks),
            mesh=split,
            in_specs=in_specs,
            out_specs=out_specs,
            check_vma=False,
        )(*args)

    return program
```

```python
import functools

import jax
import jax.numpy as jnp
from jax import lax
from jax.experimental import pallas as pl
from jax.experimental.pallas import tpu as pltpu
from jax.sharding import Mesh, PartitionSpec as P

F32 = jnp.float32
BF16 = jnp.bfloat16
MIB = 2**20


def swap(array, axis):
    return lax.ppermute(array, axis, [(0, 1), (1, 0)])


def cross(array, halves):
    return lax.ppermute(array, ("x", "core"), [(i, halves - 1 - i) for i in range(halves)])


def dot(left, right, over):
    return lax.dot_general(left, right, ((over[:1], over[1:]), ((), ())), preferred_element_type=F32)


def softmax(logits, axis):
    shifted = jnp.exp(logits - jnp.max(logits, axis=axis, keepdims=True))
    return shifted / jnp.sum(shifted, axis=axis, keepdims=True)


def softmax_back(probabilities, upstream, axis):
    inner = jnp.sum(probabilities * upstream, axis=axis, keepdims=True)
    return probabilities * (upstream - inner)


def gelu_parts(value):
    scale, cubic = 0.7978845608028654, 0.044715
    square = value * value
    curve = jnp.tanh(scale * (value + cubic * value * square))
    slope = 0.5 * (1.0 + curve) + 0.5 * value * (1.0 - curve * curve) * scale * (1.0 + 3.0 * cubic * square)
    return 0.5 * value * (1.0 + curve), slope


def inward(table, slots, lead):
    table = table.reshape(-1, slots, table.shape[1]).swapaxes(0, 1)
    table = jnp.concatenate([table[:, lead:], table[:, :lead]], axis=1)
    return table.reshape(-1, table.shape[2])


def outward(table, slots, lead):
    table = table.reshape(slots, -1, table.shape[1])
    lead = table.shape[1] - lead
    table = jnp.concatenate([table[:, lead:], table[:, :lead]], axis=1)
    return table.swapaxes(0, 1).reshape(-1, table.shape[2])


def to_blocks(forward, backward, slots, copies):
    rows = [part for table in (forward, backward) for part in jnp.split(table.astype(F32), slots)]
    blocks = jnp.stack(rows, axis=1).astype(BF16)
    return jnp.concatenate([blocks] * copies, axis=0)


def from_blocks(blocks, slots):
    rows = [blocks[:, i] for i in range(2 * slots)]
    return jnp.concatenate(rows[:slots], axis=0), jnp.concatenate(rows[slots:], axis=0)


def start_kernel(slots, lead, tokens, cotangent, params, own, params_in, logits, params_here, sems):
    copies = [
        pltpu.make_async_copy(source, target, sems.at[i])
        for i, (source, target) in enumerate(((params, params_here), (tokens, own.at[0]), (cotangent, own.at[1])))
    ]
    for copy in copies:
        copy.start()
    copies[0].wait()
    params_in[...] = inward(params_here[...].astype(F32), slots, lead).astype(BF16)
    copies[1].wait()
    logits[...] = dot(params_in[...], own[0], (1, 1))
    copies[2].wait()


def add_kernel(slots, lead, logits, tokens, params, total):
    params_in = inward(params[...].astype(F32), slots, lead).astype(BF16)
    total[...] = logits[...] + dot(params_in, tokens[...], (1, 1))


def weight_kernel(chunks, after, up_matrix, down_matrix, up_here, down_here, up_turned, sems):
    copies = []
    for i, (source, target) in enumerate(((up_matrix, up_here), (down_matrix, down_here))):
        step = source.shape[1] // chunks
        for j in range(chunks):
            part = pl.ds(j * step, step)
            copies.append(pltpu.make_async_copy(source.at[0, part], target.at[part], sems.at[i * chunks + j]))
            copies[-1].start()
    step = up_here.shape[0] // chunks
    for j in range(chunks):
        copies[j].wait()
        up_turned[:, j * step : (j + 1) * step] = up_here[j * step : (j + 1) * step].T
    for copy in copies[chunks:]:
        copy.wait()


def slot_kernel(slots, x_size, first, second, own, tokens, cotangent, blocks, dispatch, combine):
    logits = first[...] + second[...]
    over_tokens, over_columns = softmax(logits, 1), softmax(logits, 0)
    dispatch[...] = over_tokens
    combine[...] = over_columns
    quarter = own.shape[2]
    core = lax.axis_index("core")
    for part, core in (((own[0], own[1]), core), ((tokens[...], cotangent[...]), 1 - core)):
        here = pl.ds(pl.multiple_of(core * quarter, quarter), quarter)
        slot_in = dot(over_tokens.astype(BF16), part[0], (1, 0))
        grad_out = dot(over_columns.astype(BF16), part[1], (1, 0))
        blocks[:, :, here] = to_blocks(slot_in, grad_out, slots, x_size)


def expert_kernel(slots, x_size, blocks, up_matrix, down_matrix, up_turned, sums):
    got = blocks[...].astype(F32)
    first, second = jnp.split(got, x_size)
    in_order = lax.axis_index("x") != lax.axis_index("core")
    parts = (jnp.where(in_order, first, second), jnp.where(in_order, second, first))
    sides = [from_blocks(part, slots) for part in parts]
    forward, backward = (jnp.concatenate(side, axis=1).astype(BF16) for side in zip(*sides))
    preact = dot(forward, up_matrix[...], (1, 0))
    grad_hidden = dot(backward, down_matrix[...], (1, 1))
    hidden, slope = gelu_parts(preact)
    sums[0] = dot(hidden.astype(BF16), down_matrix[...], (1, 0)).astype(BF16)
    sums[1] = dot((grad_hidden * slope).astype(BF16), up_turned[...], (1, 0)).astype(BF16)


def pair_kernel(slots, x_size, first, second, blocks):
    total = first[...].astype(F32) + second[...].astype(F32)
    blocks[...] = to_blocks(total[0], total[1], slots, x_size)


def image_kernel(
    slots, x_size, lead, middle, order, blocks, own, tokens, cotangent, across, corner, dispatch, combine, params, params_part, mixed, grad_tokens, rows
):
    half = lax.axis_index("x") * 2 + lax.axis_index("core")
    quarter = own.shape[2]
    slot_out, grad_in = from_blocks(sum(jnp.split(blocks[...].astype(F32), x_size)), slots)
    rows[0] = slot_out.astype(BF16)
    rows[1] = grad_in.astype(BF16)
    grad_combine = grad_dispatch = 0.0
    for offset, part in enumerate((own, (tokens, cotangent), corner, across)):
        start = pl.multiple_of(jnp.bitwise_xor(half, offset) * quarter, quarter)
        grad_combine += dot(rows[0, :, pl.ds(start, quarter)], part[1][...], (1, 1))
        grad_dispatch += dot(rows[1, :, pl.ds(start, quarter)], part[0][...], (1, 1))
    grad_logits = softmax_back(combine[...], grad_combine, 0) + softmax_back(dispatch[...], grad_dispatch, 1)
    partial = [dot(grad_logits.astype(BF16), part[0], (1, 0)) for part in (own, (tokens[...],))]
    partial = [outward(part, slots, lead).astype(BF16) for part in partial]
    early = lax.axis_index("expert") < middle
    sides = jnp.where(early, *partial), jnp.where(early, *partial[::-1])
    for i, image in enumerate(order):
        params_part[i] = sides[0 if image < middle else 1]
    here = pl.ds(pl.multiple_of(half * quarter, quarter), quarter)
    mixed[...] = dot(combine[...].astype(BF16), rows[0, :, here], (0, 0)).astype(BF16)
    token_term = dot(dispatch[...].astype(BF16), rows[1, :, here], (0, 0))
    grad_tokens[...] = (token_term + dot(grad_logits.astype(BF16), params[...], (0, 0))).astype(BF16)


def end_kernel(parts, mixed_here, grad_tokens_here, mixed, grad_tokens, grad_params):
    mixed[...] = mixed_here[...]
    grad_tokens[...] = grad_tokens_here[...]
    grad_params[...] = jnp.sum(parts[...].astype(F32), axis=0)


def call(kernel, outs, *args, scratch=(), in_hbm=(), limit=16):
    whole = pl.BlockSpec(memory_space=pltpu.VMEM)
    elsewhere = pl.BlockSpec(memory_space=pltpu.HBM)
    run = pl.pallas_call(
        kernel,
        out_shape=[jax.ShapeDtypeStruct(*out) if isinstance(out, tuple) else out for out in outs],
        in_specs=[elsewhere if i in in_hbm else whole for i in range(len(args))],
        out_specs=[whole] * len(outs),
        scratch_shapes=list(scratch),
        compiler_params=pltpu.CompilerParams(vmem_limit_bytes=limit * MIB),
    )
    return run(*(pltpu.with_memory_space_constraint(arg, pltpu.HBM) if i in in_hbm else arg for i, arg in enumerate(args)))


def local(experts, halves, tokens, slot_params, w_up, w_down, cotangent):
    seq, quarter = tokens.shape
    columns = slot_params.shape[1]
    slots = columns // experts
    x_size = halves // 2
    width = halves * quarter
    table = (columns, seq)
    lead, middle = experts * 5 // 8, experts // 2
    order = [(lead + i) % experts for i in range(experts)]
    near = [lead] + [i for i in range(experts) if i != lead]
    wide = [
        [(expert * x_size + (x if core else 1 - x)) * 2 + core for core in (1, 0) for expert in order]
        for x in range(x_size)
    ]
    narrow = [
        [(image * x_size + x) * 2 + (side if image < middle else 1 - side) for image in near]
        for x in range(x_size)
        for side in (0, 1)
    ]
    axes = ("expert", "x", "core")

    beside = [swap(tokens, "core"), swap(cotangent, "core")]
    own, params, logits = call(
        functools.partial(start_kernel, slots, lead),
        [((2, seq, quarter), BF16), ((columns, quarter), BF16), (table, F32)],
        tokens,
        cotangent,
        slot_params.T,
        scratch=[pltpu.VMEM((columns, quarter), BF16), pltpu.SemaphoreType.DMA((3,))],
        in_hbm=(0, 1, 2),
    )
    (logits,) = call(
        functools.partial(add_kernel, slots, lead), [(table, F32)], logits, beside[0], swap(slot_params.T, "core")
    )
    other = cross(logits, halves)
    chunks = 2
    shapes = [w_up.shape[1:], w_down.shape[1:], w_up.shape[:0:-1]]
    weights = call(
        functools.partial(weight_kernel, chunks),
        [pltpu.VMEM(shape, BF16) for shape in shapes],
        logits,
        w_up,
        w_down,
        scratch=[pltpu.SemaphoreType.DMA((2 * chunks,))],
        in_hbm=(1, 2),
    )
    other, own_later, *weights = lax.optimization_barrier((other, own, *weights))
    across = cross(own_later, halves)
    blocks, dispatch, combine = call(
        functools.partial(slot_kernel, slots, x_size),
        [((x_size * experts, 2 * slots, 2 * quarter), BF16), (table, F32), (table, F32)],
        logits,
        other,
        own,
        *beside,
    )

    blocks = lax.all_to_all(blocks, axes, 0, 0, tiled=True, axis_index_groups=wide)
    (sums,) = call(
        functools.partial(expert_kernel, slots, x_size), [((2, columns, width), BF16)], blocks, *weights
    )

    sums, across = lax.optimization_barrier((sums, across))
    other_sums = swap(sums, "core")
    corner = swap(across, "core")
    (blocks,) = call(
        functools.partial(pair_kernel, slots, x_size),
        [((x_size * experts, 2 * slots, width), BF16)],
        sums,
        other_sums,
    )
    blocks, corner = lax.optimization_barrier((blocks, corner))
    blocks = lax.all_to_all(blocks, axes, 0, 0, tiled=True, axis_index_groups=wide)
    params_part, mixed, grad_tokens = call(
        functools.partial(image_kernel, slots, x_size, lead, middle, near),
        [((experts, columns, quarter), BF16), pltpu.VMEM((seq, quarter), BF16), pltpu.VMEM((seq, quarter), BF16)],
        blocks,
        own,
        *beside,
        across,
        corner,
        dispatch,
        combine,
        params,
        scratch=[pltpu.VMEM((2, columns, width), BF16)],
        limit=16 if experts * columns <= 1024 else 48,
    )

    params_parts = lax.all_to_all(params_part, axes, 0, 0, tiled=True, axis_index_groups=narrow)
    mixed, grad_tokens, grad_params = call(
        end_kernel,
        [((seq, quarter), BF16), ((seq, quarter), BF16), ((columns, quarter), F32)],
        params_parts,
        mixed,
        grad_tokens,
        limit=16 if experts * columns <= 1024 else 48,
    )
    return mixed, grad_tokens, grad_params.T


def solution(mesh):
    experts, halves = mesh.shape["expert"], mesh.shape["half"]
    split = Mesh(mesh.devices.reshape(experts, halves // 2, 2), ("expert", "x", "core"))
    half = ("x", "core")
    in_specs = (
        P("expert", half),
        P(half, None),
        P("expert", None, half),
        P("expert", half, None),
        P("expert", half),
    )
    out_specs = (P("expert", half), P("expert", half), P(half, None))

    def program(*args):
        return jax.shard_map(
            lambda *blocks: local(experts, halves, *blocks),
            mesh=split,
            in_specs=in_specs,
            out_specs=out_specs,
            check_vma=False,
        )(*args)

    return program
```

```python
import functools

import jax
import jax.numpy as jnp
from jax import lax
from jax.experimental import pallas as pl
from jax.experimental.pallas import tpu as pltpu
from jax.sharding import Mesh, PartitionSpec as P

F32 = jnp.float32
BF16 = jnp.bfloat16
MIB = 2**20


def swap(array, axis):
    return lax.ppermute(array, axis, [(0, 1), (1, 0)])


def cross(array, halves):
    return lax.ppermute(array, ("x", "core"), [(i, halves - 1 - i) for i in range(halves)])


def dot(left, right, over):
    return lax.dot_general(left, right, ((over[:1], over[1:]), ((), ())), preferred_element_type=F32)


def softmax(logits, axis):
    shifted = jnp.exp(logits - jnp.max(logits, axis=axis, keepdims=True))
    return shifted / jnp.sum(shifted, axis=axis, keepdims=True)


def softmax_back(probabilities, upstream, axis):
    inner = jnp.sum(probabilities * upstream, axis=axis, keepdims=True)
    return probabilities * (upstream - inner)


def gelu_parts(value):
    scale, cubic = 0.7978845608028654, 0.044715
    square = value * value
    curve = jnp.tanh(scale * (value + cubic * value * square))
    slope = 0.5 * (1.0 + curve) + 0.5 * value * (1.0 - curve * curve) * scale * (1.0 + 3.0 * cubic * square)
    return 0.5 * value * (1.0 + curve), slope


def inward(table, slots, lead):
    table = table.reshape(-1, slots, table.shape[1]).swapaxes(0, 1)
    table = jnp.concatenate([table[:, lead:], table[:, :lead]], axis=1)
    return table.reshape(-1, table.shape[2])


def outward(table, slots, lead):
    table = table.reshape(slots, -1, table.shape[1])
    lead = table.shape[1] - lead
    table = jnp.concatenate([table[:, lead:], table[:, :lead]], axis=1)
    return table.swapaxes(0, 1).reshape(-1, table.shape[2])


def to_blocks(forward, backward, slots, copies):
    rows = [part for table in (forward, backward) for part in jnp.split(table.astype(F32), slots)]
    blocks = jnp.stack(rows, axis=1).astype(BF16)
    return jnp.concatenate([blocks] * copies, axis=0)


def from_blocks(blocks, slots):
    rows = [blocks[:, i] for i in range(2 * slots)]
    return jnp.concatenate(rows[:slots], axis=0), jnp.concatenate(rows[slots:], axis=0)


def start_kernel(slots, lead, tokens, cotangent, params, own, params_in, logits, params_here, sems):
    copies = [
        pltpu.make_async_copy(source, target, sems.at[i])
        for i, (source, target) in enumerate(((params, params_here), (tokens, own.at[0]), (cotangent, own.at[1])))
    ]
    for copy in copies:
        copy.start()
    copies[0].wait()
    params_in[...] = inward(params_here[...].astype(F32), slots, lead).astype(BF16)
    copies[1].wait()
    logits[...] = dot(params_in[...], own[0], (1, 1))
    copies[2].wait()


def add_kernel(slots, lead, logits, tokens, params, total):
    params_in = inward(params[...].astype(F32), slots, lead).astype(BF16)
    total[...] = logits[...] + dot(params_in, tokens[...], (1, 1))


def weight_kernel(chunks, after, up_matrix, down_matrix, up_here, down_here, up_turned, sems):
    copies = []
    for i, (source, target) in enumerate(((up_matrix, up_here), (down_matrix, down_here))):
        step = source.shape[1] // chunks
        for j in range(chunks):
            part = pl.ds(j * step, step)
            copies.append(pltpu.make_async_copy(source.at[0, part], target.at[part], sems.at[i * chunks + j]))
            copies[-1].start()
    step = up_here.shape[0] // chunks
    for j in range(chunks):
        copies[j].wait()
        up_turned[:, j * step : (j + 1) * step] = up_here[j * step : (j + 1) * step].T
    for copy in copies[chunks:]:
        copy.wait()


def slot_kernel(slots, x_size, first, second, own, tokens, cotangent, blocks, dispatch, combine):
    logits = first[...] + second[...]
    over_tokens, over_columns = softmax(logits, 1), softmax(logits, 0)
    dispatch[...] = over_tokens
    combine[...] = over_columns
    quarter = own.shape[2]
    core = lax.axis_index("core")
    for part, core in (((own[0], own[1]), core), ((tokens[...], cotangent[...]), 1 - core)):
        here = pl.ds(pl.multiple_of(core * quarter, quarter), quarter)
        slot_in = dot(over_tokens.astype(BF16), part[0], (1, 0))
        grad_out = dot(over_columns.astype(BF16), part[1], (1, 0))
        blocks[:, :, here] = to_blocks(slot_in, grad_out, slots, x_size)


def expert_kernel(slots, x_size, blocks, up_matrix, down_matrix, up_turned, sums):
    got = blocks[...].astype(F32)
    first, second = jnp.split(got, x_size)
    in_order = lax.axis_index("x") != lax.axis_index("core")
    parts = (jnp.where(in_order, first, second), jnp.where(in_order, second, first))
    sides = [from_blocks(part, slots) for part in parts]
    forward, backward = (jnp.concatenate(side, axis=1).astype(BF16) for side in zip(*sides))
    preact = dot(forward, up_matrix[...], (1, 0))
    grad_hidden = dot(backward, down_matrix[...], (1, 1))
    hidden, slope = gelu_parts(preact)
    sums[0] = dot(hidden.astype(BF16), down_matrix[...], (1, 0)).astype(BF16)
    sums[1] = dot((grad_hidden * slope).astype(BF16), up_turned[...], (1, 0)).astype(BF16)


def pair_kernel(slots, x_size, first, second, blocks):
    total = first[...].astype(F32) + second[...].astype(F32)
    blocks[...] = to_blocks(total[0], total[1], slots, x_size)


def image_kernel(
    slots, x_size, lead, middle, order, blocks, own, tokens, cotangent, across, corner, dispatch, combine, params, params_part, mixed, grad_tokens, rows
):
    half = lax.axis_index("x") * 2 + lax.axis_index("core")
    quarter = own.shape[2]
    slot_out, grad_in = from_blocks(sum(jnp.split(blocks[...].astype(F32), x_size)), slots)
    rows[0] = slot_out.astype(BF16)
    rows[1] = grad_in.astype(BF16)
    grad_combine = grad_dispatch = 0.0
    for offset, part in enumerate((own, (tokens, cotangent), corner, across)):
        start = pl.multiple_of(jnp.bitwise_xor(half, offset) * quarter, quarter)
        grad_combine += dot(rows[0, :, pl.ds(start, quarter)], part[1][...], (1, 1))
        grad_dispatch += dot(rows[1, :, pl.ds(start, quarter)], part[0][...], (1, 1))
    grad_logits = softmax_back(combine[...], grad_combine, 0) + softmax_back(dispatch[...], grad_dispatch, 1)
    partial = [dot(grad_logits.astype(BF16), part[0], (1, 0)) for part in (own, (tokens[...],))]
    partial = [outward(part, slots, lead).astype(BF16) for part in partial]
    early = lax.axis_index("expert") < middle
    sides = jnp.where(early, *partial), jnp.where(early, *partial[::-1])
    for i, image in enumerate(order):
        params_part[i] = sides[0 if image < middle else 1]
    here = pl.ds(pl.multiple_of(half * quarter, quarter), quarter)
    mixed[...] = dot(combine[...].astype(BF16), rows[0, :, here], (0, 0)).astype(BF16)
    token_term = dot(dispatch[...].astype(BF16), rows[1, :, here], (0, 0))
    grad_tokens[...] = (token_term + dot(grad_logits.astype(BF16), params[...], (0, 0))).astype(BF16)


def end_kernel(parts, mixed_here, grad_tokens_here, mixed, grad_tokens, grad_params):
    mixed[...] = mixed_here[...]
    grad_tokens[...] = grad_tokens_here[...]
    grad_params[...] = jnp.sum(parts[...].astype(F32), axis=0)


def call(kernel, outs, *args, scratch=(), in_hbm=(), limit=16):
    whole = pl.BlockSpec(memory_space=pltpu.VMEM)
    elsewhere = pl.BlockSpec(memory_space=pltpu.HBM)
    run = pl.pallas_call(
        kernel,
        out_shape=[jax.ShapeDtypeStruct(*out) if isinstance(out, tuple) else out for out in outs],
        in_specs=[elsewhere if i in in_hbm else whole for i in range(len(args))],
        out_specs=[whole] * len(outs),
        scratch_shapes=list(scratch),
        compiler_params=pltpu.CompilerParams(vmem_limit_bytes=limit * MIB),
    )
    return run(*(pltpu.with_memory_space_constraint(arg, pltpu.HBM) if i in in_hbm else arg for i, arg in enumerate(args)))


def local(experts, halves, tokens, slot_params, w_up, w_down, cotangent):
    seq, quarter = tokens.shape
    columns = slot_params.shape[1]
    slots = columns // experts
    x_size = halves // 2
    width = halves * quarter
    table = (columns, seq)
    lead, middle = experts * 5 // 8, experts // 2
    order = [(lead + i) % experts for i in range(experts)]
    near = [lead] + [i for i in range(experts) if i != lead]
    wide = [
        [(expert * x_size + (x if core else 1 - x)) * 2 + core for core in (1, 0) for expert in order]
        for x in range(x_size)
    ]
    narrow = [
        [(image * x_size + x) * 2 + (side if image < middle else 1 - side) for image in near]
        for x in range(x_size)
        for side in (0, 1)
    ]
    axes = ("expert", "x", "core")

    beside = [swap(tokens, "core"), swap(cotangent, "core")]
    own, params, logits = call(
        functools.partial(start_kernel, slots, lead),
        [((2, seq, quarter), BF16), ((columns, quarter), BF16), (table, F32)],
        tokens,
        cotangent,
        slot_params.T,
        scratch=[pltpu.VMEM((columns, quarter), BF16), pltpu.SemaphoreType.DMA((3,))],
        in_hbm=(0, 1, 2),
    )
    (logits,) = call(
        functools.partial(add_kernel, slots, lead), [(table, F32)], logits, beside[0], swap(slot_params.T, "core")
    )
    other = cross(logits, halves)
    chunks = 4
    shapes = [w_up.shape[1:], w_down.shape[1:], w_up.shape[:0:-1]]
    weights = call(
        functools.partial(weight_kernel, chunks),
        [pltpu.VMEM(shape, BF16) for shape in shapes],
        logits,
        w_up,
        w_down,
        scratch=[pltpu.SemaphoreType.DMA((2 * chunks,))],
        in_hbm=(1, 2),
    )
    other, own_later, *weights = lax.optimization_barrier((other, own, *weights))
    across = cross(own_later, halves)
    blocks, dispatch, combine = call(
        functools.partial(slot_kernel, slots, x_size),
        [((x_size * experts, 2 * slots, 2 * quarter), BF16), (table, F32), (table, F32)],
        logits,
        other,
        own,
        *beside,
    )

    blocks = lax.all_to_all(blocks, axes, 0, 0, tiled=True, axis_index_groups=wide)
    (sums,) = call(
        functools.partial(expert_kernel, slots, x_size), [((2, columns, width), BF16)], blocks, *weights
    )

    sums, across = lax.optimization_barrier((sums, across))
    other_sums = swap(sums, "core")
    corner = swap(across, "core")
    (blocks,) = call(
        functools.partial(pair_kernel, slots, x_size),
        [((x_size * experts, 2 * slots, width), BF16)],
        sums,
        other_sums,
    )
    blocks, corner = lax.optimization_barrier((blocks, corner))
    blocks = lax.all_to_all(blocks, axes, 0, 0, tiled=True, axis_index_groups=wide)
    params_part, mixed, grad_tokens = call(
        functools.partial(image_kernel, slots, x_size, lead, middle, near),
        [((experts, columns, quarter), BF16), pltpu.VMEM((seq, quarter), BF16), pltpu.VMEM((seq, quarter), BF16)],
        blocks,
        own,
        *beside,
        across,
        corner,
        dispatch,
        combine,
        params,
        scratch=[pltpu.VMEM((2, columns, width), BF16)],
        limit=16 if experts * columns <= 1024 else 48,
    )

    params_parts = lax.all_to_all(params_part, axes, 0, 0, tiled=True, axis_index_groups=narrow)
    mixed, grad_tokens, grad_params = call(
        end_kernel,
        [((seq, quarter), BF16), ((seq, quarter), BF16), ((columns, quarter), F32)],
        params_parts,
        mixed,
        grad_tokens,
        limit=16 if experts * columns <= 1024 else 48,
    )
    return mixed, grad_tokens, grad_params.T


def solution(mesh):
    experts, halves = mesh.shape["expert"], mesh.shape["half"]
    split = Mesh(mesh.devices.reshape(experts, halves // 2, 2), ("expert", "x", "core"))
    half = ("x", "core")
    in_specs = (
        P("expert", half),
        P(half, None),
        P("expert", None, half),
        P("expert", half, None),
        P("expert", half),
    )
    out_specs = (P("expert", half), P("expert", half), P(half, None))

    def program(*args):
        return jax.shard_map(
            lambda *blocks: local(experts, halves, *blocks),
            mesh=split,
            in_specs=in_specs,
            out_specs=out_specs,
            check_vma=False,
        )(*args)

    return program
```

```python
import functools

import jax
import jax.numpy as jnp
from jax import lax
from jax.experimental import pallas as pl
from jax.experimental.pallas import tpu as pltpu
from jax.sharding import Mesh, PartitionSpec as P

F32 = jnp.float32
BF16 = jnp.bfloat16
MIB = 2**20


def swap(array, axis):
    return lax.ppermute(array, axis, [(0, 1), (1, 0)])


def cross(array, halves):
    return lax.ppermute(array, ("x", "core"), [(i, halves - 1 - i) for i in range(halves)])


def dot(left, right, over):
    return lax.dot_general(left, right, ((over[:1], over[1:]), ((), ())), preferred_element_type=F32)


def softmax(logits, axis):
    shifted = jnp.exp(logits - jnp.max(logits, axis=axis, keepdims=True))
    return shifted / jnp.sum(shifted, axis=axis, keepdims=True)


def softmax_back(probabilities, upstream, axis):
    inner = jnp.sum(probabilities * upstream, axis=axis, keepdims=True)
    return probabilities * (upstream - inner)


def gelu_parts(value):
    scale, cubic = 0.7978845608028654, 0.044715
    square = value * value
    curve = jnp.tanh(scale * (value + cubic * value * square))
    slope = 0.5 * (1.0 + curve) + 0.5 * value * (1.0 - curve * curve) * scale * (1.0 + 3.0 * cubic * square)
    return 0.5 * value * (1.0 + curve), slope


def inward(table, slots, lead):
    table = table.reshape(-1, slots, table.shape[1]).swapaxes(0, 1)
    table = jnp.concatenate([table[:, lead:], table[:, :lead]], axis=1)
    return table.reshape(-1, table.shape[2])


def outward(table, slots, lead):
    table = table.reshape(slots, -1, table.shape[1])
    lead = table.shape[1] - lead
    table = jnp.concatenate([table[:, lead:], table[:, :lead]], axis=1)
    return table.swapaxes(0, 1).reshape(-1, table.shape[2])


def to_blocks(forward, backward, slots, copies):
    rows = [part for table in (forward, backward) for part in jnp.split(table.astype(F32), slots)]
    blocks = jnp.stack(rows, axis=1).astype(BF16)
    return jnp.concatenate([blocks] * copies, axis=0)


def from_blocks(blocks, slots):
    rows = [blocks[:, i] for i in range(2 * slots)]
    return jnp.concatenate(rows[:slots], axis=0), jnp.concatenate(rows[slots:], axis=0)


def start_kernel(slots, lead, tokens, cotangent, params, own, params_in, logits, params_here, sems):
    copies = [
        pltpu.make_async_copy(source, target, sems.at[i])
        for i, (source, target) in enumerate(((params, params_here), (tokens, own.at[0]), (cotangent, own.at[1])))
    ]
    for copy in copies:
        copy.start()
    copies[0].wait()
    params_in[...] = inward(params_here[...].astype(F32), slots, lead).astype(BF16)
    copies[1].wait()
    logits[...] = dot(params_in[...], own[0], (1, 1))
    copies[2].wait()


def add_kernel(slots, lead, logits, tokens, params, total):
    params_in = inward(params[...].astype(F32), slots, lead).astype(BF16)
    total[...] = logits[...] + dot(params_in, tokens[...], (1, 1))


def weight_kernel(chunks, after, up_matrix, down_matrix, up_here, down_here, up_turned, sems):
    copies = []
    for i, (source, target) in enumerate(((up_matrix, up_here), (down_matrix, down_here))):
        step = source.shape[1] // chunks
        for j in range(chunks):
            part = pl.ds(j * step, step)
            copies.append(pltpu.make_async_copy(source.at[0, part], target.at[part], sems.at[i * chunks + j]))
            copies[-1].start()
    step = up_here.shape[0] // chunks
    for j in range(chunks):
        copies[j].wait()
        up_turned[:, j * step : (j + 1) * step] = up_here[j * step : (j + 1) * step].T
    for copy in copies[chunks:]:
        copy.wait()


def slot_kernel(slots, x_size, first, second, own, tokens, cotangent, blocks, dispatch, combine):
    logits = first[...] + second[...]
    over_tokens, over_columns = softmax(logits, 1), softmax(logits, 0)
    dispatch[...] = over_tokens
    combine[...] = over_columns
    quarter = own.shape[2]
    core = lax.axis_index("core")
    for part, core in (((own[0], own[1]), core), ((tokens[...], cotangent[...]), 1 - core)):
        here = pl.ds(pl.multiple_of(core * quarter, quarter), quarter)
        slot_in = dot(over_tokens.astype(BF16), part[0], (1, 0))
        grad_out = dot(over_columns.astype(BF16), part[1], (1, 0))
        blocks[:, :, here] = to_blocks(slot_in, grad_out, slots, x_size)


def expert_kernel(slots, x_size, blocks, up_matrix, down_matrix, up_turned, sums):
    got = blocks[...].astype(F32)
    first, second = jnp.split(got, x_size)
    in_order = lax.axis_index("x") != lax.axis_index("core")
    parts = (jnp.where(in_order, first, second), jnp.where(in_order, second, first))
    sides = [from_blocks(part, slots) for part in parts]
    forward, backward = (jnp.concatenate(side, axis=1).astype(BF16) for side in zip(*sides))
    preact = dot(forward, up_matrix[...], (1, 0))
    grad_hidden = dot(backward, down_matrix[...], (1, 1))
    hidden, slope = gelu_parts(preact)
    sums[0] = dot(hidden.astype(BF16), down_matrix[...], (1, 0)).astype(BF16)
    sums[1] = dot((grad_hidden * slope).astype(BF16), up_turned[...], (1, 0)).astype(BF16)


def pair_kernel(slots, x_size, first, second, blocks):
    total = first[...].astype(F32) + second[...].astype(F32)
    blocks[...] = to_blocks(total[0], total[1], slots, x_size)


def image_kernel(
    slots, x_size, lead, middle, order, blocks, own, tokens, cotangent, across, corner, dispatch, combine, params, params_part, mixed, grad_tokens, rows
):
    half = lax.axis_index("x") * 2 + lax.axis_index("core")
    quarter = own.shape[2]
    slot_out, grad_in = from_blocks(sum(jnp.split(blocks[...].astype(F32), x_size)), slots)
    rows[0] = slot_out.astype(BF16)
    rows[1] = grad_in.astype(BF16)
    grad_combine = grad_dispatch = 0.0
    for offset, part in enumerate((own, (tokens, cotangent), corner, across)):
        start = pl.multiple_of(jnp.bitwise_xor(half, offset) * quarter, quarter)
        grad_combine += dot(rows[0, :, pl.ds(start, quarter)], part[1][...], (1, 1))
        grad_dispatch += dot(rows[1, :, pl.ds(start, quarter)], part[0][...], (1, 1))
    grad_logits = softmax_back(combine[...], grad_combine, 0) + softmax_back(dispatch[...], grad_dispatch, 1)
    partial = [dot(grad_logits.astype(BF16), part[0], (1, 0)) for part in (own, (tokens[...],))]
    partial = [outward(part, slots, lead).astype(BF16) for part in partial]
    early = lax.axis_index("expert") < middle
    sides = jnp.where(early, *partial), jnp.where(early, *partial[::-1])
    for i, image in enumerate(order):
        params_part[i] = sides[0 if image < middle else 1]
    here = pl.ds(pl.multiple_of(half * quarter, quarter), quarter)
    mixed[...] = dot(combine[...].astype(BF16), rows[0, :, here], (0, 0)).astype(BF16)
    token_term = dot(dispatch[...].astype(BF16), rows[1, :, here], (0, 0))
    grad_tokens[...] = (token_term + dot(grad_logits.astype(BF16), params[...], (0, 0))).astype(BF16)


def end_kernel(parts, mixed_here, grad_tokens_here, mixed, grad_tokens, grad_params):
    mixed[...] = mixed_here[...]
    grad_tokens[...] = grad_tokens_here[...]
    grad_params[...] = jnp.sum(parts[...].astype(F32), axis=0)


def call(kernel, outs, *args, scratch=(), in_hbm=(), limit=16):
    whole = pl.BlockSpec(memory_space=pltpu.VMEM)
    elsewhere = pl.BlockSpec(memory_space=pltpu.HBM)
    run = pl.pallas_call(
        kernel,
        out_shape=[jax.ShapeDtypeStruct(*out) if isinstance(out, tuple) else out for out in outs],
        in_specs=[elsewhere if i in in_hbm else whole for i in range(len(args))],
        out_specs=[whole] * len(outs),
        scratch_shapes=list(scratch),
        compiler_params=pltpu.CompilerParams(vmem_limit_bytes=limit * MIB),
    )
    return run(*(pltpu.with_memory_space_constraint(arg, pltpu.HBM) if i in in_hbm else arg for i, arg in enumerate(args)))


def local(experts, halves, tokens, slot_params, w_up, w_down, cotangent):
    seq, quarter = tokens.shape
    columns = slot_params.shape[1]
    slots = columns // experts
    x_size = halves // 2
    width = halves * quarter
    table = (columns, seq)
    lead, middle = experts * 5 // 8, experts // 2
    order = [(lead + i) % experts for i in range(experts)]
    near = [(lead - i) % experts for i in range(experts)]
    wide = [
        [(expert * x_size + (x if core else 1 - x)) * 2 + core for core in (1, 0) for expert in order]
        for x in range(x_size)
    ]
    narrow = [
        [(image * x_size + x) * 2 + (side if image < middle else 1 - side) for image in near]
        for x in range(x_size)
        for side in (0, 1)
    ]
    axes = ("expert", "x", "core")

    beside = [swap(tokens, "core"), swap(cotangent, "core")]
    own, params, logits = call(
        functools.partial(start_kernel, slots, lead),
        [((2, seq, quarter), BF16), ((columns, quarter), BF16), (table, F32)],
        tokens,
        cotangent,
        slot_params.T,
        scratch=[pltpu.VMEM((columns, quarter), BF16), pltpu.SemaphoreType.DMA((3,))],
        in_hbm=(0, 1, 2),
    )
    (logits,) = call(
        functools.partial(add_kernel, slots, lead), [(table, F32)], logits, beside[0], swap(slot_params.T, "core")
    )
    other = cross(logits, halves)
    chunks = 2
    shapes = [w_up.shape[1:], w_down.shape[1:], w_up.shape[:0:-1]]
    weights = call(
        functools.partial(weight_kernel, chunks),
        [pltpu.VMEM(shape, BF16) for shape in shapes],
        logits,
        w_up,
        w_down,
        scratch=[pltpu.SemaphoreType.DMA((2 * chunks,))],
        in_hbm=(1, 2),
    )
    other, own_later, *weights = lax.optimization_barrier((other, own, *weights))
    across = cross(own_later, halves)
    blocks, dispatch, combine = call(
        functools.partial(slot_kernel, slots, x_size),
        [((x_size * experts, 2 * slots, 2 * quarter), BF16), (table, F32), (table, F32)],
        logits,
        other,
        own,
        *beside,
    )

    blocks = lax.all_to_all(blocks, axes, 0, 0, tiled=True, axis_index_groups=wide)
    (sums,) = call(
        functools.partial(expert_kernel, slots, x_size), [((2, columns, width), BF16)], blocks, *weights
    )

    sums, across = lax.optimization_barrier((sums, across))
    other_sums = swap(sums, "core")
    corner = swap(across, "core")
    (blocks,) = call(
        functools.partial(pair_kernel, slots, x_size),
        [((x_size * experts, 2 * slots, width), BF16)],
        sums,
        other_sums,
    )
    blocks, corner = lax.optimization_barrier((blocks, corner))
    blocks = lax.all_to_all(blocks, axes, 0, 0, tiled=True, axis_index_groups=wide)
    params_part, mixed, grad_tokens = call(
        functools.partial(image_kernel, slots, x_size, lead, middle, near),
        [((experts, columns, quarter), BF16), pltpu.VMEM((seq, quarter), BF16), pltpu.VMEM((seq, quarter), BF16)],
        blocks,
        own,
        *beside,
        across,
        corner,
        dispatch,
        combine,
        params,
        scratch=[pltpu.VMEM((2, columns, width), BF16)],
        limit=16 if experts * columns <= 1024 else 48,
    )

    params_parts = lax.all_to_all(params_part, axes, 0, 0, tiled=True, axis_index_groups=narrow)
    mixed, grad_tokens, grad_params = call(
        end_kernel,
        [((seq, quarter), BF16), ((seq, quarter), BF16), ((columns, quarter), F32)],
        params_parts,
        mixed,
        grad_tokens,
        limit=16 if experts * columns <= 1024 else 48,
    )
    return mixed, grad_tokens, grad_params.T


def solution(mesh):
    experts, halves = mesh.shape["expert"], mesh.shape["half"]
    split = Mesh(mesh.devices.reshape(experts, halves // 2, 2), ("expert", "x", "core"))
    half = ("x", "core")
    in_specs = (
        P("expert", half),
        P(half, None),
        P("expert", None, half),
        P("expert", half, None),
        P("expert", half),
    )
    out_specs = (P("expert", half), P("expert", half), P(half, None))

    def program(*args):
        return jax.shard_map(
            lambda *blocks: local(experts, halves, *blocks),
            mesh=split,
            in_specs=in_specs,
            out_specs=out_specs,
            check_vma=False,
        )(*args)

    return program
```
